128 devices in a mesh: latent: 16 (over y, z), dp: 8 (over x, core).
Axes of the slice: x: 4, y: 4, z: 4, core: 2. Of those that a mesh axis runs over, the one named last changes fastest.
Arguments:
- residual: bfloat16 [1024, 4608], P('dp', 'latent'), may hold values from -6 to 6
- encoder: bfloat16 [4608, 131072], P(None, ('latent', 'dp')), may hold values from -0.09375 to 0.09375
- encoder_bias: float32 [131072], P(('latent', 'dp')), may hold values from -3 to 3
- thresholds: int32 [131072], P(('latent', 'dp')), may hold values from 32 to 255
- decoder: bfloat16 [131072, 4608], P(('latent', 'dp')), may hold values from -0.03125 to 0.03125
- decoder_bias: float32 [4608], replicated, may hold values from -4 to 4
- probes: bfloat16 [131072, 64], P(('latent', 'dp')), may hold values from -0.03125 to 0.03125
- probe_bias: float32 [64], replicated, may hold values from -4 to 4
- labels: int32 [1024, 64], replicated, may hold values 0 or 1
Outputs:
- error: float32 [1024], P(('latent', 'dp'))
- probe_grad: float32 [131072, 64], P(('latent', 'dp'))
- bias_grad: float32 [64], replicated
- mean_loss: float32 [], replicated
The draws below stay inside these ranges and needn't reach their ends.
All inputs are finite; a program needn't handle non-finite values.
Results may differ from the reference program's by a relative error of at most 0.00075.
Values may be sent and summed in bfloat16 or wider, within the bound.
No kernel may reach another device: no remote copies, remote signals or barrier semaphores. Data moves between devices by JAX's collectives and lax.ppermute only.
A program may use at most 192 MiB of HBM per device.

```python
import jax
import jax.numpy as jnp
from jax import lax

D = 4608
LAT_DEV = 1024
PROBES = 64
TOK_GRP = 128
LATENTS = 131072
TOKENS = 1024
N_DP = 8


def touch_ends(drawn, rng, smallest, top_value):
    spot = [jax.random.randint(jax.random.fold_in(rng, axis), (), 0, length) for axis, length in enumerate(drawn.shape)]
    widest = drawn.shape.index(max(drawn.shape))
    next_to = spot[:widest] + [(spot[widest] + 1) % drawn.shape[widest]] + spot[widest + 1:]
    return drawn.at[tuple(spot)].set(smallest).at[tuple(next_to)].set(top_value)


def steps_of(stream_key, shape, shards, least, high):
    gain = 1.0
    for position, blocks in shards:
        draws = jax.random.uniform(jax.random.fold_in(jax.random.fold_in(stream_key, 6), position), (blocks,), jnp.float32, least / len(shards), high / len(shards))
        gain = gain * jnp.repeat(jnp.exp(draws), shape[position] // blocks).reshape((-1,) + (1,) * (len(shape) - 1 - position))
    return gain


def gaussian(stream_key, extent, spread, most, split=(), kind=jnp.bfloat16):
    result = spread * jax.random.normal(stream_key, extent, jnp.float32)
    if split:
        result = result * steps_of(stream_key, extent, split, -0.22, 0.18)
    return jnp.clip(result, -most, most).astype(kind)


def setup_inputs(seed: int = 0) -> dict:
    key_of = jax.random.split(jax.random.key(seed), 10)
    return {
        "residual": gaussian(key_of[0], (TOKENS, D), 1.0, 6.0, ((0, 8), (1, 16))),
        "encoder": gaussian(key_of[1], (D, LATENTS), D ** -0.5, 0.09375, ((1, 128),)),
        "encoder_bias": gaussian(key_of[2], (LATENTS,), 0.5, 3.0, ((0, 128),), jnp.float32),
        "thresholds": touch_ends(jax.random.randint(key_of[3], (LATENTS,), 32, 256), jax.random.fold_in(key_of[3], 1), 32, 255).astype(jnp.int32),
        "decoder": gaussian(key_of[4], (LATENTS, D), (LATENTS // 4) ** -0.5, 0.03125, ((0, 128),)),
        "decoder_bias": gaussian(key_of[5], (D,), 1.0, 4.0, (), jnp.float32),
        "probes": gaussian(key_of[6], (LATENTS, PROBES), (LATENTS // 4) ** -0.5, 0.03125, ((0, 128),)),
        "probe_bias": gaussian(key_of[7], (PROBES,), 1.0, 4.0, (), jnp.float32),
        "labels": touch_ends((jax.random.randint(key_of[8], (TOKENS, PROBES), 0, 2) < 1).astype(jnp.int32), jax.random.fold_in(key_of[8], 1), 0, 1),
    }


softness = 0.1
levels = 256.0

def activate(residual, encoder, encoder_bias, thresholds, first, count):
    weights = lax.dynamic_slice_in_dim(encoder, first, count, 1)
    preact = jnp.dot(residual, weights, preferred_element_type=jnp.float32)
    preact = preact + lax.dynamic_slice_in_dim(encoder_bias, first, count, 0)
    cutoff = lax.dynamic_slice_in_dim(thresholds, first, count, 0).astype(jnp.float32) / levels
    return (preact * jax.nn.sigmoid((preact - cutoff) / softness)).astype(jnp.bfloat16)

def reference(residual, encoder, encoder_bias, thresholds, decoder, decoder_bias, probes, probe_bias, labels):
    tokens = residual.shape[0]
    block_size = LAT_DEV * N_DP
    blocks = LATENTS // block_size

    def accumulate(index, carry):
        recon, logits = carry
        first = (index * block_size).astype(jnp.int32)
        active = activate(residual, encoder, encoder_bias, thresholds, first, block_size)
        recon = recon + jnp.dot(active, lax.dynamic_slice_in_dim(decoder, first, block_size, 0), preferred_element_type=jnp.float32)
        logits = logits + jnp.dot(active, lax.dynamic_slice_in_dim(probes, first, block_size, 0), preferred_element_type=jnp.float32)
        return (recon, logits)
    start = (jnp.zeros((tokens, D), jnp.float32), jnp.zeros((tokens, PROBES), jnp.float32))
    recon, logits = lax.fori_loop(0, blocks, accumulate, start)
    recon = recon + decoder_bias
    error = lax.optimization_barrier(jnp.mean((residual.astype(jnp.float32) - recon) ** 2, axis=1))
    logits = logits + probe_bias
    target = labels.astype(jnp.float32)
    slopes = (jax.nn.sigmoid(logits) - target).astype(jnp.bfloat16)
    mean_loss = jnp.sum(jax.nn.softplus(logits) - target * logits) / (tokens * PROBES)

    def block_grad(index):
        first = (index * block_size).astype(jnp.int32)
        active = activate(residual, encoder, encoder_bias, thresholds, first, block_size)
        return jnp.dot(active.T, slopes, preferred_element_type=jnp.float32) / TOK_GRP
    probe_grad = lax.map(block_grad, jnp.arange(blocks, dtype=jnp.int32)).reshape(LATENTS, PROBES)
    bias_grad = lax.optimization_barrier(jnp.sum(slopes.astype(jnp.float32), axis=0)) / TOK_GRP
    return (error, probe_grad, bias_grad, mean_loss)
```

```python
import functools

import jax
import jax.numpy as jnp
from jax import lax
from jax.experimental import pallas as pl
from jax.experimental.pallas import tpu as pltpu
from jax.sharding import PartitionSpec as P

softness = 0.1
levels = 256.0
AXES = ("latent", "dp")
F32 = jnp.float32
BF16 = jnp.bfloat16
KB = 1152
D = 4608
W = D + 128
W2 = D + 512
W3 = D + 1024
VMEM_LIMIT = 8 * 1024 * 1024


def flat(y, z, x, c):
    return ((y * 4 + z) * 4 + x) * 2 + c


def coords():
    for y in range(4):
        for z in range(4):
            for x in range(4):
                for c in range(2):
                    yield {"y": y, "z": z, "x": x}, c


def place(p, c):
    return flat(p["y"], p["z"], p["x"], c)


def pull_perm(axis0, axis1, step):
    pairs = []
    for p, c in coords():
        axis = (axis0, axis1)[c]
        q = dict(p)
        q[axis] = (p[axis] + step) % 4
        pairs.append((place(q, c), place(p, c)))
    return pairs


def pull(value, axis0, axis1, step):
    return lax.ppermute(value, AXES, pull_perm(axis0, axis1, step))


def swap(value):
    pairs = [(place(p, c), place(p, 1 - c)) for p, c in coords()]
    return lax.ppermute(value, AXES, pairs)


def absolute(parts, start):
    twice = jnp.stack(list(parts) * 2)
    return lax.dynamic_slice_in_dim(twice, lax.rem(4 - start, 4), 4, 0)


def relative(stacked, start):
    return lax.dynamic_slice_in_dim(jnp.concatenate([stacked, stacked], 0), start, 4, 0)


STAGES = (0, 1, 3, 2)


def encode_kernel(stage, count, tile, where, *refs):
    own, oth = refs[:count], refs[count : 2 * count]
    refs = refs[2 * count :]
    enc, bias, cut = refs[:3]
    acc = None if stage == STAGES[0] else refs[3]
    xa, ya = refs[-2:]
    core, y = where[0], where[1]
    depth = 4 // count

    def rows(step):
        return pl.ds(pl.multiple_of(lax.rem(y + step, 4) * KB, KB), KB)

    def work(by_x, by_y):
        @pl.loop(0, enc.shape[1] // tile)
        def _(n):
            cols = pl.ds(pl.multiple_of(n * tile, tile), tile)

            def activate(preact):
                gate = jax.nn.sigmoid((preact - cut[:, cols]) / softness)
                return (preact * gate).astype(BF16)

            pre = bias[:, cols] + sum(
                jnp.dot(
                    by_x[j // depth][j % depth], enc[rows(j), cols], preferred_element_type=F32
                )
                for j in range(4)
            )
            xa[:, cols] = activate(pre)
            for i in range(count):
                part = jnp.dot(
                    by_y[i][...].reshape(128 * depth, KB),
                    enc[rows(stage), cols],
                    preferred_element_type=F32,
                )
                span = slice(128 * depth * i, 128 * depth * (i + 1))
                if acc is not None:
                    part = part + acc[span, cols]
                if stage == STAGES[-1]:
                    ya[span, cols] = activate(part + bias[:, cols])
                else:
                    ya[span, cols] = part

    @pl.when(core == 0)
    def _():
        work(own, oth)

    @pl.when(core == 1)
    def _():
        work(oth, own)


def encode(stage, where, own, oth, enc, bias, cut, acc):
    lat = enc.shape[1]
    vmem = pl.BlockSpec(memory_space=pltpu.VMEM)
    args = [*own, *oth, enc, bias, cut]
    aliases = {}
    if acc is not None:
        args.append(acc)
        if stage != STAGES[-1]:
            aliases = {len(args): 1}
    return pl.pallas_call(
        functools.partial(encode_kernel, stage, len(own), 256),
        in_specs=[pl.BlockSpec(memory_space=pltpu.SMEM)] + [vmem] * len(args),
        out_specs=[vmem, vmem],
        out_shape=[
            jax.ShapeDtypeStruct((128, lat), BF16),
            jax.ShapeDtypeStruct((512, lat), BF16 if stage == STAGES[-1] else F32),
        ],
        input_output_aliases=aliases,
        compiler_params=pltpu.CompilerParams(vmem_limit_bytes=VMEM_LIMIT),
        cost_estimate=pl.CostEstimate(
            flops=2 * 256 * D * lat, bytes_accessed=0, transcendentals=0
        ),
        name="encode",
    )(where, *args)


def split(total):
    lane = lax.broadcasted_iota(jnp.int32, total.shape, total.ndim - 1)
    high = total.astype(BF16).astype(F32)
    return jnp.where(lane < 64, high, total - high)


def joined(pair):
    return pair + pltpu.roll(pair, 64, pair.ndim - 1)


def decode_kernel(tile, where, xa, ya, dec, probes, keep, send, lhs):
    core, pick = where[0], where[2]
    lhs[pl.ds(pl.multiple_of(core * 128, 128), 128), :] = xa[...]
    lhs[pl.ds(pl.multiple_of((1 - core) * 128, 128), 128), :] = ya[pick]
    logits = split(jnp.dot(lhs[...], probes[...], preferred_element_type=F32)).astype(BF16)
    keep[:, D:] = logits[:128]
    send[:, D:] = logits[128:]

    @pl.loop(0, D // tile)
    def _(n):
        cols = pl.ds(pl.multiple_of(n * tile, tile), tile)
        out = jnp.dot(lhs[...], dec[:, cols], preferred_element_type=F32).astype(BF16)
        keep[:, cols] = out[:128]
        send[:, cols] = out[128:]


def decode(where, xa, ya, dec, probes):
    lat = dec.shape[0]
    vmem = pl.BlockSpec(memory_space=pltpu.VMEM)
    return pl.pallas_call(
        functools.partial(decode_kernel, 768),
        in_specs=[pl.BlockSpec(memory_space=pltpu.SMEM)] + [vmem] * 4,
        out_specs=[vmem, vmem],
        scratch_shapes=[pltpu.VMEM((256, lat), BF16)],
        out_shape=[jax.ShapeDtypeStruct((128, W), BF16)] * 2,
        compiler_params=pltpu.CompilerParams(vmem_limit_bytes=VMEM_LIMIT),
        cost_estimate=pl.CostEstimate(
            flops=2 * 256 * D * lat, bytes_accessed=0, transcendentals=0
        ),
        name="decode",
    )(where, xa, ya, dec, probes)


def small_call(kernel, name, outs, *args, scalars=1, scratch=()):
    vmem = pl.BlockSpec(memory_space=pltpu.VMEM)
    smem = pl.BlockSpec(memory_space=pltpu.SMEM)
    return pl.pallas_call(
        kernel,
        in_specs=[smem] * scalars + [vmem] * (len(args) - scalars),
        out_specs=[vmem] * len(outs),
        out_shape=[jax.ShapeDtypeStruct(shape, kind) for shape, kind in outs],
        scratch_shapes=list(scratch),
        compiler_params=pltpu.CompilerParams(vmem_limit_bytes=VMEM_LIMIT),
        name=name,
    )(*args)


def pair_kernel(a, b, out):
    out[:, :D] = (a[:, :D].astype(F32) + b[:, :D].astype(F32)).astype(BF16)
    total = joined(a[:, D:].astype(F32) + b[:, D:].astype(F32))
    out[:, D:] = split(total).astype(BF16)


def pair_sum(a, b):
    return small_call(pair_kernel, "pair_sum", [((128, W), BF16)], a, b, scalars=0)[0]


def first_kernel(where, a0, b0, g1, g2, g3, *outs):
    spot = where[3]
    logits = sum(r[:, D:].astype(F32) for r in (a0, b0, g1, g2, g3))
    logits = split(joined(logits)).astype(BF16)
    for d, out in enumerate(outs):
        rows = pl.ds(pl.multiple_of(lax.rem(spot + d, 4) * 32, 32), 32)
        out[:, :D] = sum(r[rows, :D].astype(F32) for r in (a0, b0, g1, g2, g3)).astype(BF16)
        for k in range(4):
            out[:, D + 128 * k : D + 128 * (k + 1)] = logits[32 * k : 32 * (k + 1)]


def second_kernel(where, m0, g1, g2, g3, *refs):
    outs, total, wide = refs[:4], refs[4], refs[5]
    spot = where[4]

    def four(cols):
        a0, a1, a2, a3 = (r[:, cols].astype(F32) for r in (m0, g1, g2, g3))
        return (a0 + a2) + (a1 + a3)

    total[...] = four(slice(0, D))
    for k in range(4):
        cols = slice(D + 128 * k, D + 128 * (k + 1))
        l0, l1, l2, l3 = (joined(r[:, cols].astype(F32)) for r in (m0, g1, g2, g3))
        wide[32 * k : 32 * (k + 1), :] = (l0 + l2) + (l1 + l3)
    lane = lax.broadcasted_iota(jnp.int32, (8, 128), 1)
    packed = [
        jnp.where(lane < 64, wide[8 * i : 8 * i + 8, :], wide[64 + 8 * i : 72 + 8 * i, :])
        for i in range(8)
    ]
    for d, out in enumerate(outs):
        rows = pl.ds(pl.multiple_of(lax.rem(spot + d, 4) * 8, 8), 8)
        out[:, :D] = total[rows, :]
        for i in range(8):
            out[:, D + 128 * i : D + 128 * (i + 1)] = packed[i]


def third_kernel(m0, g1, g2, g3, tokens, bias, err, logits):
    def four(cols):
        a0, a1, a2, a3 = (r[:, cols] for r in (m0, g1, g2, g3))
        return (a0 + a2) + (a1 + a3)

    gap = tokens[...] - (four(slice(0, D)) + bias[...])
    err[...] = jnp.broadcast_to(jnp.sum(gap * gap, axis=1, keepdims=True) / D, err.shape)
    logits[...] = four(slice(D, W3))


def on_device(
    residual, encoder, encoder_bias, thresholds, decoder, decoder_bias, probes, probe_bias, labels
):
    per_group = residual.shape[0]
    lat = encoder.shape[1]
    pos = lax.axis_index(AXES)
    core = pos % 2
    x, z, y = (pos // 2) % 4, (pos // 8) % 4, pos // 32
    is0 = core == 0
    first = jnp.where(is0, x, y)
    second = jnp.where(is0, y, z)
    third = jnp.where(is0, z, x)

    parts = [residual] + [pull(residual, "z", "z", d) for d in (1, 2, 3)]
    unit = absolute(parts, z).transpose(1, 0, 2).reshape(per_group, KB)
    block = jnp.stack([unit] + [pull(unit, "y", "x", d) for d in (1, 2, 3)])
    own, oth = {0: [block]}, {0: [swap(block)]}
    near = {d: pull(block, "x", "y", d) for d in (1, 3)}

    cut = (thresholds.astype(F32) / levels)[None]
    bias = encoder_bias[None]
    where = jnp.stack([core, y]).astype(jnp.int32)
    xa = {}

    def run(stage, acc):
        xa[stage], acc = encode(stage, where, own[stage], oth[stage], encoder, bias, cut, acc)
        return acc

    acc = run(0, None)
    near, acc = lax.optimization_barrier((near, acc))
    far = [pull(near[1][:2], "x", "y", 1), pull(near[3][2:], "x", "y", 3)]
    for d in (1, 3):
        own[d], oth[d] = [near[d]], [swap(near[d])]
    acc = run(1, acc)
    acc = run(3, acc)
    far, acc = lax.optimization_barrier((far, acc))
    own[2], oth[2] = far, [swap(half) for half in far]
    acc = run(2, acc)
    ya = acc.reshape(4, 128, lat)

    probes2 = jnp.concatenate([probes, probes], axis=1)
    order = (2, 1, 3, 0)
    keep, got, message = {}, {}, {}
    for i, d in enumerate(order):
        spot = jnp.stack([core, y, lax.rem(y + d - x + 4, 4)]).astype(jnp.int32)
        left = xa[d]
        if i >= 2:
            left, message[order[i - 2]] = lax.optimization_barrier((left, message[order[i - 2]]))
        keep[d], send = decode(spot, left, ya, decoder, probes2)
        got[d] = swap(send)
        if d:
            message[d] = pair_sum(keep[d], got[d])
    mine = {d: pull(message[d], "x", "y", 4 - d) for d in (2, 1, 3)}

    where = jnp.stack([core, y, core, second, third]).astype(jnp.int32)
    m2 = small_call(
        first_kernel, "first_sum", [((32, W2), BF16)] * 4,
        where, keep[0], got[0], mine[1], mine[2], mine[3],
    )
    g2 = [pull(m2[d], "y", "z", 4 - d) for d in (1, 2, 3)]
    m3 = small_call(
        second_kernel, "second_sum", [((8, W3), F32)] * 4, where, m2[0], *g2,
        scratch=[pltpu.VMEM((32, D), F32), pltpu.VMEM((128, 128), F32)],
    )
    g3 = [pull(m3[d], "z", "x", 4 - d) for d in (1, 2, 3)]

    start = second * 32 + third * 8
    by_x = lax.dynamic_slice(block, (0, start, 0), (4, 8, KB))
    turn = lax.rem(y - x + 4, 4)

    def at(part, index):
        return lax.dynamic_slice(part, (index, start, 0), (1, 8, KB))

    low, high = at(far[0], jnp.minimum(turn, 1)), at(far[1], jnp.maximum(turn - 2, 0))
    by_y = jnp.concatenate(
        [at(block, turn), at(near[1], turn), jnp.where(turn < 2, low, high), at(near[3], turn)]
    )
    chosen = jnp.where(is0, by_x, by_y).astype(F32)
    tokens = relative(chosen, lax.rem(4 - y, 4)).transpose(1, 0, 2).reshape(8, D)

    err, packed = small_call(
        third_kernel, "third_sum", [((8, 128), F32), ((8, 1024), F32)],
        m3[0], *g3, tokens, decoder_bias[None], scalars=0,
    )
    owners = []
    for p, c in coords():
        s = (p["x"], p["y"], p["z"]) if c == 0 else (p["y"], p["z"], p["x"])
        owners.append((place(p, c), s[0] * 32 + c * 16 + s[1] * 4 + s[2]))
    error = lax.ppermute(err, AXES, owners)[:, 0]

    mine = absolute([packed] + [pull(packed, "x", "y", d) for d in (1, 2, 3)], first)
    theirs = swap(mine)
    both = jnp.stack([jnp.where(is0, mine, theirs), jnp.where(is0, theirs, mine)], 1)
    both = both.reshape(4, 2, 8, 8, 2, 64).transpose(0, 1, 4, 3, 2, 5).reshape(4, 2, 128, 64)
    logits = both + probe_bias
    target = labels.astype(F32).reshape(4, 2, 128, 64)
    slopes = (jax.nn.sigmoid(logits) - target).astype(BF16)
    mean_loss = jnp.sum(jax.nn.softplus(logits) - target * logits) / target.size
    bias_grad = jnp.sum(slopes.astype(F32), axis=(0, 1, 2)) / per_group
    turned = relative(slopes, x)
    active = jnp.concatenate([xa[0], xa[1], xa[2], xa[3], ya.reshape(512, lat)])
    turned = turned.transpose(1, 0, 2, 3).reshape(1024, 64)
    probe_grad = (
        lax.dot_general(active, turned, (((0,), (0,)), ((), ())), preferred_element_type=F32)
        / per_group
    )
    return (error, probe_grad, bias_grad, mean_loss)


def solution(mesh):
    in_specs = (
        P("dp", "latent"),
        P(None, ("latent", "dp")),
        P(("latent", "dp")),
        P(("latent", "dp")),
        P(("latent", "dp"), None),
        P(),
        P(("latent", "dp"), None),
        P(),
        P(),
    )
    out_specs = (P(("latent", "dp")), P(("latent", "dp"), None), P(), P())
    return jax.shard_map(
        on_device, mesh=mesh, in_specs=in_specs, out_specs=out_specs, check_vma=False
    )
```

```python
import functools

import jax
import jax.numpy as jnp
from jax import lax
from jax.experimental import pallas as pl
from jax.experimental.pallas import tpu as pltpu
from jax.sharding import PartitionSpec as P

softness = 0.1
levels = 256.0
AXES = ("latent", "dp")
F32 = jnp.float32
BF16 = jnp.bfloat16
KB = 1152
D = 4608
W = D + 128
W2 = D + 512
W3 = D + 1024
VMEM_LIMIT = 8 * 1024 * 1024
LITTLE = pl.CostEstimate(flops=1000000, bytes_accessed=0, transcendentals=0)


def flat(y, z, x, c):
    return ((y * 4 + z) * 4 + x) * 2 + c


def coords():
    for y in range(4):
        for z in range(4):
            for x in range(4):
                for c in range(2):
                    yield {"y": y, "z": z, "x": x}, c


def place(p, c):
    return flat(p["y"], p["z"], p["x"], c)


def pull_perm(axis0, axis1, step):
    pairs = []
    for p, c in coords():
        axis = (axis0, axis1)[c]
        q = dict(p)
        q[axis] = (p[axis] + step) % 4
        pairs.append((place(q, c), place(p, c)))
    return pairs


def pull(value, axis0, axis1, step):
    return lax.ppermute(value, AXES, pull_perm(axis0, axis1, step))


def swap(value):
    pairs = [(place(p, c), place(p, 1 - c)) for p, c in coords()]
    return lax.ppermute(value, AXES, pairs)


def absolute(parts, start):
    twice = jnp.stack(list(parts) * 2)
    return lax.dynamic_slice_in_dim(twice, lax.rem(4 - start, 4), 4, 0)


def load_kernel(source, target, sems):
    pieces = sems.shape[0]
    rows = source.shape[0] // pieces
    copies = []
    for i in range(pieces):
        span = slice(rows * i, rows * (i + 1))
        copies.append(pltpu.make_async_copy(source.at[span], target.at[span], sems.at[i]))
    for copy in copies:
        copy.start()
    for copy in copies:
        copy.wait()


def load(value):
    held = pl.pallas_call(
        load_kernel,
        in_specs=[pl.BlockSpec(memory_space=pltpu.HBM)],
        out_specs=pl.BlockSpec(memory_space=pltpu.VMEM),
        out_shape=jax.ShapeDtypeStruct(value.shape, value.dtype),
        scratch_shapes=[pltpu.SemaphoreType.DMA((4,))],
        compiler_params=pltpu.CompilerParams(vmem_limit_bytes=VMEM_LIMIT),
        cost_estimate=LITTLE,
        name="load",
    )(pltpu.with_memory_space_constraint(value, pltpu.HBM))
    return near(held)


def near(value):
    return pltpu.with_memory_space_constraint(value, pltpu.VMEM)


STAGES = (0, 1, 3, 2)


def encode_kernel(stage, count, tile, where, *refs):
    core, y = where[0], where[2]
    own, oth = refs[:count], refs[count : 2 * count]
    refs = refs[2 * count :]
    enc, bias, cut = refs[:3]
    acc = None if stage == STAGES[0] else refs[3]
    xa, ya = refs[-2:]
    depth = 4 // count

    def rows(step):
        return pl.ds(pl.multiple_of(lax.rem(y + step, 4) * KB, KB), KB)

    def work(by_x, by_y):
        @pl.loop(0, enc.shape[1] // tile)
        def _(n):
            cols = pl.ds(pl.multiple_of(n * tile, tile), tile)

            def activate(preact):
                cutoff = cut[:, cols].astype(F32) / levels
                gate = jax.nn.sigmoid((preact - cutoff) / softness)
                return (preact * gate).astype(BF16)

            pre = bias[:, cols] + sum(
                jnp.dot(
                    by_x[j // depth][j % depth], enc[rows(j), cols], preferred_element_type=F32
                )
                for j in range(4)
            )
            xa[:, cols] = activate(pre)
            for i in range(count):
                part = jnp.dot(
                    by_y[i][...].reshape(128 * depth, KB),
                    enc[rows(stage), cols],
                    preferred_element_type=F32,
                )
                span = slice(128 * depth * i, 128 * depth * (i + 1))
                if acc is not None:
                    part = part + acc[span, cols]
                if stage == STAGES[-1]:
                    ya[span, cols] = activate(part + bias[:, cols])
                else:
                    ya[span, cols] = part

    @pl.when(core == 0)
    def _():
        work(own, oth)

    @pl.when(core == 1)
    def _():
        work(oth, own)


def encode(stage, where, own, oth, enc, bias, cut, acc):
    lat = enc.shape[1]
    vmem = pl.BlockSpec(memory_space=pltpu.VMEM)
    args = [*own, *oth, enc, bias, cut]
    aliases = {}
    if acc is not None:
        args.append(acc)
        if stage != STAGES[-1]:
            aliases = {len(args): 1}
    return pl.pallas_call(
        functools.partial(encode_kernel, stage, len(own), 256),
        in_specs=[pl.BlockSpec(memory_space=pltpu.SMEM)] + [vmem] * len(args),
        out_specs=[vmem, vmem],
        out_shape=[
            jax.ShapeDtypeStruct((128, lat), BF16),
            jax.ShapeDtypeStruct((512, lat), BF16 if stage == STAGES[-1] else F32),
        ],
        input_output_aliases=aliases,
        compiler_params=pltpu.CompilerParams(vmem_limit_bytes=VMEM_LIMIT),
        cost_estimate=LITTLE,
        name="encode",
    )(where, *args)


def split(total):
    lane = lax.broadcasted_iota(jnp.int32, total.shape, total.ndim - 1)
    high = total.astype(BF16).astype(F32)
    return jnp.where(lane < 64, high, total - high)


def joined(pair):
    return pair + pltpu.roll(pair, 64, pair.ndim - 1)


def decode_kernel(step, tile, where, xa, ya, dec, probes, keep, send, lhs):
    core = where[0]
    pick = lax.rem(where[2] + step - where[1] + 4, 4)
    lhs[pl.ds(pl.multiple_of(core * 128, 128), 128), :] = xa[...]
    lhs[pl.ds(pl.multiple_of((1 - core) * 128, 128), 128), :] = ya[pick]
    logits = split(jnp.dot(lhs[...], probes[...], preferred_element_type=F32)).astype(BF16)
    keep[:, D:] = logits[:128]
    send[:, D:] = logits[128:]

    @pl.loop(0, D // tile)
    def _(n):
        cols = pl.ds(pl.multiple_of(n * tile, tile), tile)
        out = jnp.dot(lhs[...], dec[:, cols], preferred_element_type=F32).astype(BF16)
        keep[:, cols] = out[:128]
        send[:, cols] = out[128:]


def decode(step, where, xa, ya, dec, probes):
    lat = dec.shape[0]
    vmem = pl.BlockSpec(memory_space=pltpu.VMEM)
    return pl.pallas_call(
        functools.partial(decode_kernel, step, 768),
        in_specs=[pl.BlockSpec(memory_space=pltpu.SMEM)] + [vmem] * 4,
        out_specs=[vmem, vmem],
        scratch_shapes=[pltpu.VMEM((256, lat), BF16)],
        out_shape=[jax.ShapeDtypeStruct((128, W), BF16)] * 2,
        compiler_params=pltpu.CompilerParams(vmem_limit_bytes=VMEM_LIMIT),
        cost_estimate=LITTLE,
        name="decode",
    )(where, xa, ya, dec, probes)


def small_call(kernel, name, outs, *args, scalars=1, scratch=()):
    vmem = pl.BlockSpec(memory_space=pltpu.VMEM)
    smem = pl.BlockSpec(memory_space=pltpu.SMEM)
    return pl.pallas_call(
        kernel,
        in_specs=[smem] * scalars + [vmem] * (len(args) - scalars),
        out_specs=[vmem] * len(outs),
        out_shape=[jax.ShapeDtypeStruct(shape, kind) for shape, kind in outs],
        scratch_shapes=list(scratch),
        compiler_params=pltpu.CompilerParams(vmem_limit_bytes=VMEM_LIMIT),
        cost_estimate=LITTLE,
        name=name,
    )(*args)


def pair_kernel(shift, a, b, *refs):
    total = a[:, D:].astype(F32) + b[:, D:].astype(F32)
    if shift is None:
        for i, out in enumerate(refs):
            rows = slice(64 * i, 64 * (i + 1))
            out[:, :D] = (a[rows, :D].astype(F32) + b[rows, :D].astype(F32)).astype(BF16)
            out[:, D:] = split(joined(total[rows])).astype(BF16)
        return
    through, out = refs
    for i in range(2):
        rows = slice(64 * i, 64 * (i + 1))
        part = a[rows, :D].astype(F32) + b[rows, :D].astype(F32)
        logits = total[rows]
        if i == shift:
            part = part + through[:, :D].astype(F32)
            logits = logits + through[:, D:].astype(F32)
        out[rows, :D] = part.astype(BF16)
        out[rows, D:] = split(joined(logits)).astype(BF16)


def pair_sum(shift, *args):
    outs = [((64, W), BF16)] * 2 if shift is None else [((128, W), BF16)]
    kernel = functools.partial(pair_kernel, shift)
    return small_call(kernel, "pair_sum", outs, *args, scalars=0)


def first_kernel(where, a0, b0, g1, g3, *outs):
    spot = where[5]
    logits = sum(r[:, D:].astype(F32) for r in (a0, b0, g1, g3))
    logits = split(joined(logits)).astype(BF16)
    for d, out in enumerate(outs):
        rows = pl.ds(pl.multiple_of(lax.rem(spot + d, 4) * 32, 32), 32)
        out[:, :D] = sum(r[rows, :D].astype(F32) for r in (a0, b0, g1, g3)).astype(BF16)
        for k in range(4):
            out[:, D + 128 * k : D + 128 * (k + 1)] = logits[32 * k : 32 * (k + 1)]


def second_kernel(where, m0, g1, g2, g3, *refs):
    outs, total, wide = refs[:4], refs[4], refs[5]
    spot = where[6]

    def four(cols):
        a0, a1, a2, a3 = (r[:, cols].astype(F32) for r in (m0, g1, g2, g3))
        return (a0 + a2) + (a1 + a3)

    total[...] = four(slice(0, D))
    for k in range(4):
        cols = slice(D + 128 * k, D + 128 * (k + 1))
        l0, l1, l2, l3 = (joined(r[:, cols].astype(F32)) for r in (m0, g1, g2, g3))
        wide[32 * k : 32 * (k + 1), :] = (l0 + l2) + (l1 + l3)
    lane = lax.broadcasted_iota(jnp.int32, (8, 128), 1)
    packed = [
        jnp.where(lane < 64, wide[8 * i : 8 * i + 8, :], wide[64 + 8 * i : 72 + 8 * i, :])
        for i in range(8)
    ]
    for d, out in enumerate(outs):
        rows = pl.ds(pl.multiple_of(lax.rem(spot + d, 4) * 8, 8), 8)
        out[:, :D] = total[rows, :]
        for i in range(8):
            out[:, D + 128 * i : D + 128 * (i + 1)] = packed[i]


def third_kernel(m0, g1, g2, g3, tokens, bias, err, logits):
    def four(cols):
        a0, a1, a2, a3 = (r[:, cols] for r in (m0, g1, g2, g3))
        return (a0 + a2) + (a1 + a3)

    gap = tokens[...] - (four(slice(0, D)) + bias[...])
    err[...] = jnp.broadcast_to(jnp.sum(gap * gap, axis=1, keepdims=True) / D, err.shape)
    logits[...] = four(slice(D, W3))


def collect_kernel(*refs):
    for i, ref in enumerate(refs[:4]):
        refs[4][i] = ref[...]


def collect(parts):
    shape = (4, *parts[0].shape)
    return small_call(collect_kernel, "collect", [(shape, parts[0].dtype)], *parts, scalars=0)[0]


def settle_kernel(source, target):
    target[...] = source[...]


def settle(value):
    outs = [(value.shape, value.dtype)]
    return small_call(settle_kernel, "settle", outs, value, scalars=0)[0]


def halves_kernel(a, b, low, high):
    low[...] = a[:2]
    high[...] = b[2:]


def halves(a, b):
    shape = (2, *a.shape[1:])
    outs = [(shape, a.dtype)] * 2
    return small_call(halves_kernel, "halves", outs, a, b, scalars=0)


def rows_kernel(where, block, side1, low, high, side3, out, wide):
    core, x, y = where[0], where[1], where[2]
    start = where[5] * 32 + where[6] * 8
    even = pl.ds(pl.multiple_of(start // 16 * 16, 16), 16)
    turn = lax.rem(y - x + 4, 4)

    def put(j, value):
        wide[...] = value.astype(F32)
        rows = pl.ds(pl.multiple_of(lax.rem(start, 16), 8), 8)
        out[:, pl.ds(pl.multiple_of(lax.rem(y + j, 4) * KB, 128), KB)] = wide[rows, :]

    @pl.when(core == 0)
    def _():
        for j in range(4):
            put(j, block[j, even, :])

    @pl.when(core == 1)
    def _():
        put(0, block[turn, even, :])
        put(1, side1[turn, even, :])
        put(3, side3[turn, even, :])

        @pl.when(turn < 2)
        def _():
            put(2, low[jnp.minimum(turn, 1), even, :])

        @pl.when(turn >= 2)
        def _():
            put(2, high[jnp.maximum(turn - 2, 0), even, :])


def finish_kernel(groups, where, own, oth, labels, bias, *refs):
    actives, ya = refs[:4], refs[4]
    grad, bias_grad, loss, logits, slopes = refs[5:]
    core, x, y = where[0], where[1], where[2]
    lane = lax.broadcasted_iota(jnp.int32, (8, 128), 1)

    def unpack(source, start, parity):
        for d in range(4):
            g = lax.rem(start + d, 4) * 2 + parity
            for i in range(8):
                tile = source[d, :, 128 * i : 128 * (i + 1)]
                logits[g, 8 * i : 8 * i + 8, :] = tile
                logits[g, 64 + 8 * i : 72 + 8 * i, :] = pltpu.roll(tile, 64, 1)

    @pl.when(core == 0)
    def _():
        unpack(own, x, 0)
        unpack(oth, y, 1)

    @pl.when(core == 1)
    def _():
        unpack(oth, x, 0)
        unpack(own, y, 1)

    slopes[...] = jnp.zeros_like(slopes)
    total = jnp.zeros((128, 64), F32)
    sums = jnp.zeros((1, 64), F32)
    for g in range(groups):
        value = logits[g, :, :64] + bias[...]
        target = labels[128 * g : 128 * (g + 1), :].astype(F32)
        slope = (jax.nn.sigmoid(value) - target).astype(BF16)
        slopes[g, :, :64] = slope
        total = total + (jax.nn.softplus(value) - target * value)
        sums = sums + jnp.sum(slope.astype(F32), axis=0, keepdims=True)
    loss[...] = jnp.broadcast_to(
        jnp.sum(jnp.sum(total, axis=1, keepdims=True), axis=0, keepdims=True) / (groups * 128 * 64),
        loss.shape,
    )
    bias_grad[...] = sums / 128

    turned = jnp.zeros((128, ya.shape[2]), F32)
    for d in range(4):
        g = lax.rem(x + d, 4) * 2
        for active, slope in ((actives[d][...], slopes[g]), (ya[d], slopes[g + 1])):
            turned = turned + lax.dot_general(
                slope, active, (((0,), (0,)), ((), ())), preferred_element_type=F32
            )
    grad[...] = (turned / 128)[:64]


def on_device(
    residual, encoder, encoder_bias, thresholds, decoder, decoder_bias, probes, probe_bias, labels
):
    per_group = residual.shape[0]
    lat = encoder.shape[1]
    pos = lax.axis_index(AXES)
    core = pos % 2
    x, z, y = (pos // 2) % 4, (pos // 8) % 4, pos // 32
    is0 = core == 0
    first = jnp.where(is0, x, y)
    second = jnp.where(is0, y, z)
    third = jnp.where(is0, z, x)
    where = jnp.stack([core, x, y, z, first, second, third]).astype(jnp.int32)
    probes2 = jnp.concatenate([probes, probes], axis=1)

    parts = [residual] + [pull(residual, "z", "z", d) for d in (1, 2, 3)]
    unit = absolute(parts, z).transpose(1, 0, 2).reshape(per_group, KB)
    unit, where, probes2, encoder, decoder = lax.optimization_barrier(
        (unit, where, probes2, encoder, decoder)
    )
    unit = settle(unit)
    unit, encoder, decoder = lax.optimization_barrier((unit, encoder, decoder))
    encoder, decoder = load(encoder), load(decoder)
    pulled = [pull(unit, "y", "x", d) for d in (1, 2, 3)]
    unit, pulled, encoder, decoder = lax.optimization_barrier((unit, pulled, encoder, decoder))
    block = collect([unit, *pulled])
    own, oth = {0: [block]}, {0: [swap(block)]}
    sides = {d: pull(block, "x", "y", d) for d in (1, 3)}

    cut = thresholds[None]
    bias = encoder_bias[None]
    xa = {}

    def run(stage, acc):
        xa[stage], acc = encode(stage, where, own[stage], oth[stage], encoder, bias, cut, acc)
        return acc

    acc = run(0, None)
    sides, acc = lax.optimization_barrier((sides, acc))
    low, high = halves(sides[1], sides[3])
    far = [pull(low, "x", "y", 1), pull(high, "x", "y", 3)]
    for d in (1, 3):
        own[d], oth[d] = [sides[d]], [swap(sides[d])]
    acc = run(1, acc)
    acc = run(3, acc)
    far, acc = lax.optimization_barrier((far, acc))
    own[2], oth[2] = far, [swap(half) for half in far]
    acc = run(2, acc)
    ya = acc.reshape(4, 128, lat)

    keep, got = {}, {}

    def part(d, left):
        keep[d], send = decode(d, where, left, ya, decoder, probes2)
        got[d] = swap(send)

    part(2, xa[2])
    over = pair_sum(None, keep[2], got[2])
    over, left0, left1 = lax.optimization_barrier((over, xa[0], xa[1]))
    through = [pull(over[0], "x", "y", 3), pull(over[1], "x", "y", 1)]
    part(0, left0)
    part(1, left1)
    through, keep[0], keep[1], left3 = lax.optimization_barrier(
        (through, keep[0], keep[1], xa[3])
    )
    part(3, left3)
    (message1,) = pair_sum(0, keep[1], got[1], through[0])
    (message3,) = pair_sum(1, keep[3], got[3], through[1])
    mine = {1: pull(message1, "x", "y", 3), 3: pull(message3, "x", "y", 1)}
    (tokens,) = small_call(
        rows_kernel, "own_rows", [((8, D), F32)],
        where, block, sides[1], *far, sides[3], scratch=[pltpu.VMEM((16, KB), F32)],
    )

    m2 = small_call(
        first_kernel, "first_sum", [((32, W2), BF16)] * 4,
        where, keep[0], got[0], mine[1], mine[3],
    )
    g2 = [pull(m2[d], "y", "z", 4 - d) for d in (1, 2, 3)]
    m3 = small_call(
        second_kernel, "second_sum", [((8, W3), F32)] * 4, where, m2[0], *g2,
        scratch=[pltpu.VMEM((32, D), F32), pltpu.VMEM((128, 128), F32)],
    )
    g3 = [pull(m3[d], "z", "x", 4 - d) for d in (1, 2, 3)]
    err, packed = small_call(
        third_kernel, "third_sum", [((8, 128), F32), ((8, 1024), F32)],
        m3[0], *g3, tokens, decoder_bias[None], scalars=0,
    )
    owners = []
    for p, c in coords():
        s = (p["x"], p["y"], p["z"]) if c == 0 else (p["y"], p["z"], p["x"])
        owners.append((place(p, c), s[0] * 32 + c * 16 + s[1] * 4 + s[2]))

    mine = collect([packed] + [pull(packed, "x", "y", d) for d in (1, 2, 3)])
    theirs = swap(mine)
    error = lax.ppermute(err, AXES, owners)[:, 0]
    probe_grad, bias_grad, mean_loss = small_call(
        functools.partial(finish_kernel, 8), "finish",
        [((64, lat), F32), ((1, 64), F32), ((1, 128), F32)],
        where, mine, theirs, labels, probe_bias[None], xa[0], xa[1], xa[2], xa[3], ya,
        scratch=[pltpu.VMEM((8, 128, 128), F32), pltpu.VMEM((8, 128, 128), BF16)],
    )
    return (error, probe_grad.T, bias_grad[0], mean_loss[0, 0])


def solution(mesh):
    in_specs = (
        P("dp", "latent"),
        P(None, ("latent", "dp")),
        P(("latent", "dp")),
        P(("latent", "dp")),
        P(("latent", "dp"), None),
        P(),
        P(("latent", "dp"), None),
        P(),
        P(),
    )
    out_specs = (P(("latent", "dp")), P(("latent", "dp"), None), P(), P())
    return jax.shard_map(
        on_device, mesh=mesh, in_specs=in_specs, out_specs=out_specs, check_vma=False
    )
```

```python
import functools

import jax
import jax.numpy as jnp
from jax import lax
from jax.experimental import pallas as pl
from jax.experimental.pallas import tpu as pltpu
from jax.sharding import PartitionSpec as P

softness = 0.1
levels = 256.0
AXES = ("latent", "dp")
F32 = jnp.float32
BF16 = jnp.bfloat16
KB = 1152
D = 4608
W = D + 128
WR = W + 256
W2 = D + 512
C = D // 2
W3 = D + 1024
VMEM_LIMIT = 8 * 1024 * 1024
LITTLE = pl.CostEstimate(flops=1000000, bytes_accessed=0, transcendentals=0)


def flat(y, z, x, c):
    return ((y * 4 + z) * 4 + x) * 2 + c


def coords():
    for y in range(4):
        for z in range(4):
            for x in range(4):
                for c in range(2):
                    yield {"y": y, "z": z, "x": x}, c


def place(p, c):
    return flat(p["y"], p["z"], p["x"], c)


def pull_perm(axis0, axis1, step):
    pairs = []
    for p, c in coords():
        axis = (axis0, axis1)[c]
        q = dict(p)
        q[axis] = (p[axis] + step) % 4
        pairs.append((place(q, c), place(p, c)))
    return pairs


def pull(value, axis0, axis1, step):
    return lax.ppermute(value, AXES, pull_perm(axis0, axis1, step))


def swap(value):
    pairs = [(place(p, c), place(p, 1 - c)) for p, c in coords()]
    return lax.ppermute(value, AXES, pairs)


def absolute(parts, start):
    twice = jnp.stack(list(parts) * 2)
    return lax.dynamic_slice_in_dim(twice, lax.rem(4 - start, 4), 4, 0)


def load_kernel(source, target, sems):
    pieces = sems.shape[0]
    rows = source.shape[0] // pieces
    copies = []
    for i in range(pieces):
        span = slice(rows * i, rows * (i + 1))
        copies.append(pltpu.make_async_copy(source.at[span], target.at[span], sems.at[i]))
    for copy in copies:
        copy.start()
    for copy in copies:
        copy.wait()


def load(value):
    held = pl.pallas_call(
        load_kernel,
        in_specs=[pl.BlockSpec(memory_space=pltpu.HBM)],
        out_specs=pl.BlockSpec(memory_space=pltpu.VMEM),
        out_shape=jax.ShapeDtypeStruct(value.shape, value.dtype),
        scratch_shapes=[pltpu.SemaphoreType.DMA((4,))],
        compiler_params=pltpu.CompilerParams(vmem_limit_bytes=VMEM_LIMIT),
        cost_estimate=LITTLE,
        name="load",
    )(pltpu.with_memory_space_constraint(value, pltpu.HBM))
    return near(held)


def near(value):
    return pltpu.with_memory_space_constraint(value, pltpu.VMEM)


STAGES = (0, 1, 3, 2)


def encode_kernel(stage, which, tile, where, *refs):
    count = 1 if which is None else 2
    blocks = refs[: 2 * count if which is None else count]
    refs = refs[len(blocks) :]
    enc, bias, cut = refs[:3]
    acc = None if stage == STAGES[0] else refs[3]
    xa, ya = refs[-2:]
    core, y = where[0], where[2]
    depth = 4 // count

    def rows(step):
        return pl.ds(pl.multiple_of(lax.rem(y + step, 4) * KB, KB), KB)

    def activate(preact, cols):
        cutoff = cut[:, cols].astype(F32) / levels
        gate = jax.nn.sigmoid((preact - cutoff) / softness)
        return (preact * gate).astype(BF16)

    def few(parts):
        for n in range(enc.shape[1] // tile):
            cols = slice(tile * n, tile * (n + 1))
            pre = bias[:, cols] + sum(
                jnp.dot(
                    parts[j // depth][j % depth], enc[rows(j), cols], preferred_element_type=F32
                )
                for j in range(4)
            )
            xa[:, cols] = activate(pre, cols)

    def many(parts):
        for n in range(enc.shape[1] // tile):
            cols = slice(tile * n, tile * (n + 1))
            for i in range(count):
                part = jnp.dot(
                    parts[i][...].reshape(128 * depth, KB),
                    enc[rows(stage), cols],
                    preferred_element_type=F32,
                )
                span = slice(128 * depth * i, 128 * depth * (i + 1))
                if acc is not None:
                    part = part + acc[span, cols]
                if stage == STAGES[-1]:
                    ya[span, cols] = activate(part + bias[:, cols], cols)
                else:
                    ya[span, cols] = part

    for turn in (0, 1):

        @pl.when(core == turn)
        def _(turn=turn):
            if which is None:
                few([blocks[turn]])
                many([blocks[1 - turn]])
            elif which == turn:
                few(blocks)
            else:
                many(blocks)


def encode(stage, which, where, blocks, enc, bias, cut, acc, done=()):
    lat = enc.shape[1]
    vmem = pl.BlockSpec(memory_space=pltpu.VMEM)
    args = [*blocks, enc, bias, cut]
    aliases = {}
    if acc is not None:
        args.append(acc)
        if stage != STAGES[-1]:
            aliases = {len(args): 1}
    for i, value in enumerate(done):
        args.append(value)
        aliases[len(args)] = i
    return pl.pallas_call(
        functools.partial(encode_kernel, stage, which, 256),
        in_specs=[pl.BlockSpec(memory_space=pltpu.SMEM)] + [vmem] * len(args),
        out_specs=[vmem, vmem],
        out_shape=[
            jax.ShapeDtypeStruct((128, lat), BF16),
            jax.ShapeDtypeStruct((512, lat), BF16 if stage == STAGES[-1] else F32),
        ],
        input_output_aliases=aliases,
        compiler_params=pltpu.CompilerParams(vmem_limit_bytes=VMEM_LIMIT),
        cost_estimate=LITTLE,
        name="encode",
    )(where, *args)


def split(total):
    lane = lax.broadcasted_iota(jnp.int32, total.shape, total.ndim - 1)
    high = total.astype(BF16).astype(F32)
    return jnp.where(lane < 64, high, total - high)


def joined(pair):
    return pair + pltpu.roll(pair, 64, pair.ndim - 1)


def decode_kernel(step, tile, where, xa, ya, dec, probes, keep, send0, send1, lhs):
    core = where[0]
    pick = lax.rem(where[2] + step - where[1] + 4, 4)
    lhs[pl.ds(pl.multiple_of(core * 128, 128), 128), :] = xa[...]
    lhs[pl.ds(pl.multiple_of((1 - core) * 128, 128), 128), :] = ya[pick]
    logits = split(jnp.dot(lhs[...], probes[...], preferred_element_type=F32)).astype(BF16)
    keep[:, D:] = logits[:128]
    send1[:, C:] = logits[128:]

    for n in range(D // tile):
        cols = slice(tile * n, tile * (n + 1))
        send, start = (send0, tile * n) if tile * n < C else (send1, tile * n - C)
        out = jnp.dot(lhs[...], dec[:, cols], preferred_element_type=F32).astype(BF16)
        keep[:, cols] = out[:128]
        send[:, start : start + tile] = out[128:]


def decode(step, where, xa, ya, dec, probes):
    lat = dec.shape[0]
    vmem = pl.BlockSpec(memory_space=pltpu.VMEM)
    return pl.pallas_call(
        functools.partial(decode_kernel, step, 768),
        in_specs=[pl.BlockSpec(memory_space=pltpu.SMEM)] + [vmem] * 4,
        out_specs=[vmem] * 3,
        scratch_shapes=[pltpu.VMEM((256, lat), BF16)],
        out_shape=[jax.ShapeDtypeStruct((128, w), BF16) for w in (W, C, W - C)],
        compiler_params=pltpu.CompilerParams(vmem_limit_bytes=VMEM_LIMIT),
        cost_estimate=LITTLE,
        name="decode",
    )(where, xa, ya, dec, probes)


def small_call(kernel, name, outs, *args, scalars=1, scratch=()):
    vmem = pl.BlockSpec(memory_space=pltpu.VMEM)
    smem = pl.BlockSpec(memory_space=pltpu.SMEM)
    return pl.pallas_call(
        kernel,
        in_specs=[smem] * scalars + [vmem] * (len(args) - scalars),
        out_specs=[vmem] * len(outs),
        out_shape=[jax.ShapeDtypeStruct(shape, kind) for shape, kind in outs],
        scratch_shapes=list(scratch),
        compiler_params=pltpu.CompilerParams(vmem_limit_bytes=VMEM_LIMIT),
        cost_estimate=LITTLE,
        name=name,
    )(*args)


def pair_kernel(shift, a, b0, b1, *refs):
    low, high = slice(0, C), slice(C, D)
    outs = refs if shift is None else refs[1:]
    for i in range(2):
        rows = slice(64 * i, 64 * (i + 1))
        out, spot = (outs[i], slice(0, 64)) if shift is None else (outs[0], rows)
        for cols, other in ((low, b0[rows]), (high, b1[rows, :C])):
            part = a[rows, cols].astype(F32) + other.astype(F32)
            if i == shift:
                part = part + refs[0][:, cols].astype(F32)
            out[spot, cols] = part.astype(BF16)
        logits = a[rows, D:].astype(F32) + b1[rows, C:].astype(F32)
        if i == shift:
            logits = logits + refs[0][:, D:W].astype(F32)
        out[spot, D:W] = split(joined(logits)).astype(BF16)
        if shift is None:
            out[:, W:] = jnp.zeros((64, WR - W), BF16)


def pair_sum(shift, *args):
    outs = [((64, WR), BF16)] * 2 if shift is None else [((128, W), BF16)]
    kernel = functools.partial(pair_kernel, shift)
    return small_call(kernel, "pair_sum", outs, *args, scalars=0)


def first_kernel(where, a0, b0, b1, g1, g3, *outs):
    spot = where[5]
    logits = b1[:, C:].astype(F32) + sum(r[:, D:].astype(F32) for r in (a0, g1, g3))
    logits = split(joined(logits)).astype(BF16)
    for d, out in enumerate(outs):
        rows = pl.ds(pl.multiple_of(lax.rem(spot + d, 4) * 32, 32), 32)
        for cols, other in ((slice(0, C), b0[rows, :]), (slice(C, D), b1[rows, :C])):
            part = other.astype(F32) + sum(r[rows, cols].astype(F32) for r in (a0, g1, g3))
            out[:, cols] = part.astype(BF16)
        for k in range(4):
            out[:, D + 128 * k : D + 128 * (k + 1)] = logits[32 * k : 32 * (k + 1)]


def second_kernel(where, m0, g1, g2, g3, *refs):
    outs, total, wide = refs[:4], refs[4], refs[5]
    spot = where[6]

    def four(cols):
        a0, a1, a2, a3 = (r[:, cols].astype(F32) for r in (m0, g1, g2, g3))
        return (a0 + a2) + (a1 + a3)

    total[...] = four(slice(0, D))
    for k in range(4):
        cols = slice(D + 128 * k, D + 128 * (k + 1))
        l0, l1, l2, l3 = (joined(r[:, cols].astype(F32)) for r in (m0, g1, g2, g3))
        wide[32 * k : 32 * (k + 1), :] = (l0 + l2) + (l1 + l3)
    lane = lax.broadcasted_iota(jnp.int32, (8, 128), 1)
    packed = [
        jnp.where(lane < 64, wide[8 * i : 8 * i + 8, :], wide[64 + 8 * i : 72 + 8 * i, :])
        for i in range(8)
    ]
    for d, out in enumerate(outs):
        rows = pl.ds(pl.multiple_of(lax.rem(spot + d, 4) * 8, 8), 8)
        out[:, :D] = total[rows, :]
        for i in range(8):
            out[:, D + 128 * i : D + 128 * (i + 1)] = packed[i]


def third_kernel(m0, g1, g2, g3, tokens, bias, err, logits):
    def four(cols):
        a0, a1, a2, a3 = (r[:, cols] for r in (m0, g1, g2, g3))
        return (a0 + a2) + (a1 + a3)

    gap = tokens[...] - (four(slice(0, D)) + bias[...])
    err[...] = jnp.broadcast_to(jnp.sum(gap * gap, axis=1, keepdims=True) / D, err.shape)
    logits[...] = four(slice(D, W3))


def collect_kernel(*refs):
    for i, ref in enumerate(refs[:4]):
        refs[4][i] = ref[...]


def collect(parts):
    shape = (4, *parts[0].shape)
    return small_call(collect_kernel, "collect", [(shape, parts[0].dtype)], *parts, scalars=0)[0]


def settle_kernel(source, target):
    target[...] = source[...]


def settle(value):
    outs = [(value.shape, value.dtype)]
    return small_call(settle_kernel, "settle", outs, value, scalars=0)[0]


def halves_kernel(a, b, low, high):
    low[...] = a[:2]
    high[...] = b[2:]


def halves(a, b):
    shape = (2, *a.shape[1:])
    outs = [(shape, a.dtype)] * 2
    return small_call(halves_kernel, "halves", outs, a, b, scalars=0)


def rows_kernel(where, block, side1, low, high, side3, out, wide):
    core, x, y = where[0], where[1], where[2]
    start = where[5] * 32 + where[6] * 8
    even = pl.ds(pl.multiple_of(start // 16 * 16, 16), 16)
    turn = lax.rem(y - x + 4, 4)

    def put(j, value):
        wide[...] = value.astype(F32)
        rows = pl.ds(pl.multiple_of(lax.rem(start, 16), 8), 8)
        out[:, pl.ds(pl.multiple_of(lax.rem(y + j, 4) * KB, 128), KB)] = wide[rows, :]

    @pl.when(core == 0)
    def _():
        for j in range(4):
            put(j, block[j, even, :])

    @pl.when(core == 1)
    def _():
        put(0, block[turn, even, :])
        put(1, side1[turn, even, :])
        put(3, side3[turn, even, :])

        @pl.when(turn < 2)
        def _():
            put(2, low[jnp.minimum(turn, 1), even, :])

        @pl.when(turn >= 2)
        def _():
            put(2, high[jnp.maximum(turn - 2, 0), even, :])


def finish_kernel(groups, where, own, oth, labels, bias, *refs):
    actives, ya = refs[:4], refs[4]
    grad, bias_grad, loss, logits, slopes = refs[5:]
    core, x, y = where[0], where[1], where[2]
    lane = lax.broadcasted_iota(jnp.int32, (8, 128), 1)

    def unpack(source, start, parity):
        for d in range(4):
            g = lax.rem(start + d, 4) * 2 + parity
            for i in range(8):
                tile = source[d, :, 128 * i : 128 * (i + 1)]
                logits[g, 8 * i : 8 * i + 8, :] = tile
                logits[g, 64 + 8 * i : 72 + 8 * i, :] = pltpu.roll(tile, 64, 1)

    @pl.when(core == 0)
    def _():
        unpack(own, x, 0)
        unpack(oth, y, 1)

    @pl.when(core == 1)
    def _():
        unpack(oth, x, 0)
        unpack(own, y, 1)

    slopes[...] = jnp.zeros_like(slopes)
    total = jnp.zeros((128, 64), F32)
    sums = jnp.zeros((1, 64), F32)
    for g in range(groups):
        value = logits[g, :, :64] + bias[...]
        target = labels[128 * g : 128 * (g + 1), :].astype(F32)
        slope = (jax.nn.sigmoid(value) - target).astype(BF16)
        slopes[g, :, :64] = slope
        total = total + (jax.nn.softplus(value) - target * value)
        sums = sums + jnp.sum(slope.astype(F32), axis=0, keepdims=True)
    loss[...] = jnp.broadcast_to(
        jnp.sum(jnp.sum(total, axis=1, keepdims=True), axis=0, keepdims=True) / (groups * 128 * 64),
        loss.shape,
    )
    bias_grad[...] = sums / 128

    turned = jnp.zeros((128, ya.shape[2]), F32)
    for d in range(4):
        g = lax.rem(x + d, 4) * 2
        for active, slope in ((actives[d][...], slopes[g]), (ya[d], slopes[g + 1])):
            turned = turned + lax.dot_general(
                slope, active, (((0,), (0,)), ((), ())), preferred_element_type=F32
            )
    grad[...] = (turned / 128)[:64]


def on_device(
    residual, encoder, encoder_bias, thresholds, decoder, decoder_bias, probes, probe_bias, labels
):
    per_group = residual.shape[0]
    lat = encoder.shape[1]
    pos = lax.axis_index(AXES)
    core = pos % 2
    x, z, y = (pos // 2) % 4, (pos // 8) % 4, pos // 32
    is0 = core == 0
    first = jnp.where(is0, x, y)
    second = jnp.where(is0, y, z)
    third = jnp.where(is0, z, x)
    where = jnp.stack([core, x, y, z, first, second, third]).astype(jnp.int32)
    probes2 = jnp.concatenate([probes, probes], axis=1)

    parts = [residual] + [pull(residual, "z", "z", d) for d in (1, 2, 3)]
    unit = absolute(parts, z).transpose(1, 0, 2).reshape(per_group, KB)
    unit, where, probes2, encoder, decoder = lax.optimization_barrier(
        (unit, where, probes2, encoder, decoder)
    )
    unit = settle(unit)
    unit, encoder, decoder = lax.optimization_barrier((unit, encoder, decoder))
    encoder, decoder = load(encoder), load(decoder)
    pulled = [pull(unit, "y", "x", d) for d in (1, 2, 3)]
    unit, pulled, encoder, decoder = lax.optimization_barrier((unit, pulled, encoder, decoder))
    block = collect([unit, *pulled])
    other = swap(block)
    sides = {d: pull(block, "x", "y", d) for d in (1, 3)}

    cut = thresholds[None]
    bias = encoder_bias[None]
    xa = {}

    def run(stage, blocks, acc):
        xa[stage], acc = encode(stage, None, where, blocks, encoder, bias, cut, acc)
        return acc

    acc = run(0, [block, other], None)
    sides, acc = lax.optimization_barrier((sides, acc))
    low, high = halves(sides[1], sides[3])
    far = [pull(low, "x", "y", 1), pull(high, "x", "y", 3)]
    acc = run(1, [sides[1], swap(sides[1])], acc)
    acc = run(3, [sides[3], swap(sides[3])], acc)
    far, acc = lax.optimization_barrier((far, acc))
    mixed = encode(2, 0, where, far, encoder, bias, cut, acc)
    others = [swap(half) for half in far]
    xa[2], acc = encode(2, 1, where, others, encoder, bias, cut, acc, mixed)
    ya = acc.reshape(4, 128, lat)

    keep, got = {}, {}

    def part(d, left):
        keep[d], *send = decode(d, where, left, ya, decoder, probes2)
        got[d] = [swap(half) for half in send]

    part(2, xa[2])
    over = pair_sum(None, keep[2], *got[2])
    over, left1, left3 = lax.optimization_barrier((over, xa[1], xa[3]))
    through = [pull(over[0], "x", "y", 3), pull(over[1], "x", "y", 1)]
    part(1, left1)
    part(3, left3)
    through, keep[1], keep[3], left0 = lax.optimization_barrier(
        (through, keep[1], keep[3], xa[0])
    )
    (message1,) = pair_sum(0, keep[1], *got[1], through[0])
    (message3,) = pair_sum(1, keep[3], *got[3], through[1])
    message1, message3, left0 = lax.optimization_barrier((message1, message3, left0))
    part(0, left0)
    mine = {1: pull(message1, "x", "y", 3), 3: pull(message3, "x", "y", 1)}
    (tokens,) = small_call(
        rows_kernel, "own_rows", [((8, D), F32)],
        where, block, sides[1], *far, sides[3], scratch=[pltpu.VMEM((16, KB), F32)],
    )

    m2 = small_call(
        first_kernel, "first_sum", [((32, W2), BF16)] * 4,
        where, keep[0], *got[0], mine[1], mine[3],
    )
    g2 = [pull(m2[d], "y", "z", 4 - d) for d in (1, 2, 3)]
    m3 = small_call(
        second_kernel, "second_sum", [((8, W3), F32)] * 4, where, m2[0], *g2,
        scratch=[pltpu.VMEM((32, D), F32), pltpu.VMEM((128, 128), F32)],
    )
    g3 = [pull(m3[d], "z", "x", 4 - d) for d in (1, 2, 3)]
    err, packed = small_call(
        third_kernel, "third_sum", [((8, 128), F32), ((8, 1024), F32)],
        m3[0], *g3, tokens, decoder_bias[None], scalars=0,
    )
    owners = []
    for p, c in coords():
        s = (p["x"], p["y"], p["z"]) if c == 0 else (p["y"], p["z"], p["x"])
        owners.append((place(p, c), s[0] * 32 + c * 16 + s[1] * 4 + s[2]))

    pulled = [pull(packed, "x", "y", d) for d in (1, 2, 3)]
    err = lax.ppermute(err, AXES, owners)
    pulled, packed, err = lax.optimization_barrier((pulled, packed, err))
    mine = collect([packed, *pulled])
    theirs = swap(mine)
    error = err[:, 0]
    probe_grad, bias_grad, mean_loss = small_call(
        functools.partial(finish_kernel, 8), "finish",
        [((64, lat), F32), ((1, 64), F32), ((1, 128), F32)],
        where, mine, theirs, labels, probe_bias[None], xa[0], xa[1], xa[2], xa[3], ya,
        scratch=[pltpu.VMEM((8, 128, 128), F32), pltpu.VMEM((8, 128, 128), BF16)],
    )
    return (error, probe_grad.T, bias_grad[0], mean_loss[0, 0])


def solution(mesh):
    in_specs = (
        P("dp", "latent"),
        P(None, ("latent", "dp")),
        P(("latent", "dp")),
        P(("latent", "dp")),
        P(("latent", "dp"), None),
        P(),
        P(("latent", "dp"), None),
        P(),
        P(),
    )
    out_specs = (P(("latent", "dp")), P(("latent", "dp"), None), P(), P())
    return jax.shard_map(
        on_device, mesh=mesh, in_specs=in_specs, out_specs=out_specs, check_vma=False
    )
```

```python
import functools

import jax
import jax.numpy as jnp
from jax import lax
from jax.experimental import pallas as pl
from jax.experimental.pallas import tpu as pltpu
from jax.sharding import PartitionSpec as P

softness = 0.1
levels = 256.0
AXES = ("latent", "dp")
F32 = jnp.float32
BF16 = jnp.bfloat16
KB = 1152
D = 4608
W = D + 128
WR = W + 256
W2 = D + 512
C = D // 2
W3 = D + 1024
VMEM_LIMIT = 8 * 1024 * 1024
LITTLE = pl.CostEstimate(flops=1000000, bytes_accessed=0, transcendentals=0)


def flat(y, z, x, c):
    return ((y * 4 + z) * 4 + x) * 2 + c


def coords():
    for y in range(4):
        for z in range(4):
            for x in range(4):
                for c in range(2):
                    yield {"y": y, "z": z, "x": x}, c


def place(p, c):
    return flat(p["y"], p["z"], p["x"], c)


def pull_perm(axis0, axis1, step):
    pairs = []
    for p, c in coords():
        axis = (axis0, axis1)[c]
        q = dict(p)
        q[axis] = (p[axis] + step) % 4
        pairs.append((place(q, c), place(p, c)))
    return pairs


def pull(value, axis0, axis1, step):
    return lax.ppermute(value, AXES, pull_perm(axis0, axis1, step))


def swap(value):
    pairs = [(place(p, c), place(p, 1 - c)) for p, c in coords()]
    return lax.ppermute(value, AXES, pairs)


def absolute(parts, start):
    twice = jnp.stack(list(parts) * 2)
    return lax.dynamic_slice_in_dim(twice, lax.rem(4 - start, 4), 4, 0)


def load_kernel(source, target, sems):
    pieces = sems.shape[0]
    rows = source.shape[0] // pieces
    copies = []
    for i in range(pieces):
        span = slice(rows * i, rows * (i + 1))
        copies.append(pltpu.make_async_copy(source.at[span], target.at[span], sems.at[i]))
    for copy in copies:
        copy.start()
    for copy in copies:
        copy.wait()


def load(value):
    held = pl.pallas_call(
        load_kernel,
        in_specs=[pl.BlockSpec(memory_space=pltpu.HBM)],
        out_specs=pl.BlockSpec(memory_space=pltpu.VMEM),
        out_shape=jax.ShapeDtypeStruct(value.shape, value.dtype),
        scratch_shapes=[pltpu.SemaphoreType.DMA((4,))],
        compiler_params=pltpu.CompilerParams(vmem_limit_bytes=VMEM_LIMIT),
        cost_estimate=LITTLE,
        name="load",
    )(pltpu.with_memory_space_constraint(value, pltpu.HBM))
    return near(held)


def near(value):
    return pltpu.with_memory_space_constraint(value, pltpu.VMEM)


STAGES = (0, 1, 3, 2)


def encode_kernel(stage, which, tile, where, *refs):
    count = 1 if which is None else 2
    blocks = refs[: 2 * count if which is None else count]
    refs = refs[len(blocks) :]
    enc, bias, cut = refs[:3]
    acc = None if stage == STAGES[0] else refs[3]
    xa, ya = refs[-2:]
    core, y = where[0], where[2]
    depth = 4 // count

    def rows(step):
        return pl.ds(pl.multiple_of(lax.rem(y + step, 4) * KB, KB), KB)

    def activate(preact, cols):
        cutoff = cut[:, cols].astype(F32) / levels
        gate = jax.nn.sigmoid((preact - cutoff) / softness)
        return (preact * gate).astype(BF16)

    def tiles(work):
        @pl.loop(0, enc.shape[1] // tile)
        def _(n):
            work(pl.ds(pl.multiple_of(n * tile, tile), tile))

    def few(parts):
        def work(cols):
            pre = bias[:, cols] + sum(
                jnp.dot(
                    parts[j // depth][j % depth], enc[rows(j), cols], preferred_element_type=F32
                )
                for j in range(4)
            )
            xa[:, cols] = activate(pre, cols)

        tiles(work)

    def many(parts):
        def work(cols):
            for i in range(count):
                part = jnp.dot(
                    parts[i][...].reshape(128 * depth, KB),
                    enc[rows(stage), cols],
                    preferred_element_type=F32,
                )
                span = slice(128 * depth * i, 128 * depth * (i + 1))
                if acc is not None:
                    part = part + acc[span, cols]
                if stage == STAGES[-1]:
                    ya[span, cols] = activate(part + bias[:, cols], cols)
                else:
                    ya[span, cols] = part

        tiles(work)

    for turn in (0, 1):

        @pl.when(core == turn)
        def _(turn=turn):
            if which is None:
                few([blocks[turn]])
                many([blocks[1 - turn]])
            elif which == turn:
                few(blocks)
            else:
                many(blocks)


def encode(stage, which, where, blocks, enc, bias, cut, acc, done=()):
    lat = enc.shape[1]
    vmem = pl.BlockSpec(memory_space=pltpu.VMEM)
    args = [*blocks, enc, bias, cut]
    aliases = {}
    if acc is not None:
        args.append(acc)
        if stage != STAGES[-1]:
            aliases = {len(args): 1}
    for i, value in enumerate(done):
        args.append(value)
        aliases[len(args)] = i
    return pl.pallas_call(
        functools.partial(encode_kernel, stage, which, 256),
        in_specs=[pl.BlockSpec(memory_space=pltpu.SMEM)] + [vmem] * len(args),
        out_specs=[vmem, vmem],
        out_shape=[
            jax.ShapeDtypeStruct((128, lat), BF16),
            jax.ShapeDtypeStruct((512, lat), BF16 if stage == STAGES[-1] else F32),
        ],
        input_output_aliases=aliases,
        compiler_params=pltpu.CompilerParams(vmem_limit_bytes=VMEM_LIMIT),
        cost_estimate=LITTLE,
        name="encode",
    )(where, *args)


def split(total):
    lane = lax.broadcasted_iota(jnp.int32, total.shape, total.ndim - 1)
    high = total.astype(BF16).astype(F32)
    return jnp.where(lane < 64, high, total - high)


def joined(pair):
    return pair + pltpu.roll(pair, 64, pair.ndim - 1)


def decode_kernel(step, tile, where, xa, ya, dec, probes, keep, send0, send1, lhs):
    core = where[0]
    pick = lax.rem(where[2] + step - where[1] + 4, 4)
    lhs[pl.ds(pl.multiple_of(core * 128, 128), 128), :] = xa[...]
    lhs[pl.ds(pl.multiple_of((1 - core) * 128, 128), 128), :] = ya[pick]
    logits = split(jnp.dot(lhs[...], probes[...], preferred_element_type=F32)).astype(BF16)
    keep[:, D:] = logits[:128]
    send1[:, C:] = logits[128:]

    for n in range(D // tile):
        cols = slice(tile * n, tile * (n + 1))
        send, start = (send0, tile * n) if tile * n < C else (send1, tile * n - C)
        out = jnp.dot(lhs[...], dec[:, cols], preferred_element_type=F32).astype(BF16)
        keep[:, cols] = out[:128]
        send[:, start : start + tile] = out[128:]


def decode(step, where, xa, ya, dec, probes):
    lat = dec.shape[0]
    vmem = pl.BlockSpec(memory_space=pltpu.VMEM)
    return pl.pallas_call(
        functools.partial(decode_kernel, step, 768),
        in_specs=[pl.BlockSpec(memory_space=pltpu.SMEM)] + [vmem] * 4,
        out_specs=[vmem] * 3,
        scratch_shapes=[pltpu.VMEM((256, lat), BF16)],
        out_shape=[jax.ShapeDtypeStruct((128, w), BF16) for w in (W, C, W - C)],
        compiler_params=pltpu.CompilerParams(vmem_limit_bytes=VMEM_LIMIT),
        cost_estimate=LITTLE,
        name="decode",
    )(where, xa, ya, dec, probes)


def small_call(kernel, name, outs, *args, scalars=1, scratch=()):
    vmem = pl.BlockSpec(memory_space=pltpu.VMEM)
    smem = pl.BlockSpec(memory_space=pltpu.SMEM)
    return pl.pallas_call(
        kernel,
        in_specs=[smem] * scalars + [vmem] * (len(args) - scalars),
        out_specs=[vmem] * len(outs),
        out_shape=[jax.ShapeDtypeStruct(shape, kind) for shape, kind in outs],
        scratch_shapes=list(scratch),
        compiler_params=pltpu.CompilerParams(vmem_limit_bytes=VMEM_LIMIT),
        cost_estimate=LITTLE,
        name=name,
    )(*args)


def pair_kernel(shift, a, b0, b1, *refs):
    low, high = slice(0, C), slice(C, D)
    outs = refs if shift is None else refs[1:]
    for i in range(2):
        rows = slice(64 * i, 64 * (i + 1))
        out, spot = (outs[i], slice(0, 64)) if shift is None else (outs[0], rows)
        for cols, other in ((low, b0[rows]), (high, b1[rows, :C])):
            part = a[rows, cols].astype(F32) + other.astype(F32)
            if i == shift:
                part = part + refs[0][:, cols].astype(F32)
            out[spot, cols] = part.astype(BF16)
        logits = a[rows, D:].astype(F32) + b1[rows, C:].astype(F32)
        if i == shift:
            logits = logits + refs[0][:, D:W].astype(F32)
        out[spot, D:W] = split(joined(logits)).astype(BF16)
        if shift is None:
            out[:, W:] = jnp.zeros((64, WR - W), BF16)


def pair_sum(shift, *args):
    outs = [((64, WR), BF16)] * 2 if shift is None else [((128, W), BF16)]
    kernel = functools.partial(pair_kernel, shift)
    return small_call(kernel, "pair_sum", outs, *args, scalars=0)


def first_kernel(where, a0, b0, b1, g1, g3, *outs):
    spot = where[5]
    logits = b1[:, C:].astype(F32) + sum(r[:, D:].astype(F32) for r in (a0, g1, g3))
    logits = split(joined(logits)).astype(BF16)
    for d, out in enumerate(outs):
        rows = pl.ds(pl.multiple_of(lax.rem(spot + d, 4) * 32, 32), 32)
        for cols, other in ((slice(0, C), b0[rows, :]), (slice(C, D), b1[rows, :C])):
            part = other.astype(F32) + sum(r[rows, cols].astype(F32) for r in (a0, g1, g3))
            out[:, cols] = part.astype(BF16)
        for k in range(4):
            out[:, D + 128 * k : D + 128 * (k + 1)] = logits[32 * k : 32 * (k + 1)]


def second_kernel(where, m0, g1, g2, g3, *refs):
    outs, total, wide = refs[:4], refs[4], refs[5]
    spot = where[6]

    def four(cols):
        a0, a1, a2, a3 = (r[:, cols].astype(F32) for r in (m0, g1, g2, g3))
        return (a0 + a2) + (a1 + a3)

    total[...] = four(slice(0, D))
    for k in range(4):
        cols = slice(D + 128 * k, D + 128 * (k + 1))
        l0, l1, l2, l3 = (joined(r[:, cols].astype(F32)) for r in (m0, g1, g2, g3))
        wide[32 * k : 32 * (k + 1), :] = (l0 + l2) + (l1 + l3)
    lane = lax.broadcasted_iota(jnp.int32, (8, 128), 1)
    packed = [
        jnp.where(lane < 64, wide[8 * i : 8 * i + 8, :], wide[64 + 8 * i : 72 + 8 * i, :])
        for i in range(8)
    ]
    for d, out in enumerate(outs):
        rows = pl.ds(pl.multiple_of(lax.rem(spot + d, 4) * 8, 8), 8)
        out[:, :D] = total[rows, :]
        for i in range(8):
            out[:, D + 128 * i : D + 128 * (i + 1)] = packed[i]


def third_kernel(m0, g1, g2, g3, tokens, bias, err, logits):
    def four(cols):
        a0, a1, a2, a3 = (r[:, cols] for r in (m0, g1, g2, g3))
        return (a0 + a2) + (a1 + a3)

    gap = tokens[...] - (four(slice(0, D)) + bias[...])
    err[...] = jnp.broadcast_to(jnp.sum(gap * gap, axis=1, keepdims=True) / D, err.shape)
    logits[...] = four(slice(D, W3))


def collect_kernel(*refs):
    for i, ref in enumerate(refs[:4]):
        refs[4][i] = ref[...]


def collect(parts):
    shape = (4, *parts[0].shape)
    return small_call(collect_kernel, "collect", [(shape, parts[0].dtype)], *parts, scalars=0)[0]


def settle_kernel(source, target):
    target[...] = source[...]


def settle(value):
    outs = [(value.shape, value.dtype)]
    return small_call(settle_kernel, "settle", outs, value, scalars=0)[0]


def halves_kernel(a, b, low, high):
    low[...] = a[:2]
    high[...] = b[2:]


def halves(a, b):
    shape = (2, *a.shape[1:])
    outs = [(shape, a.dtype)] * 2
    return small_call(halves_kernel, "halves", outs, a, b, scalars=0)


def rows_kernel(where, block, side1, low, high, side3, out, wide):
    core, x, y = where[0], where[1], where[2]
    start = where[5] * 32 + where[6] * 8
    even = pl.ds(pl.multiple_of(start // 16 * 16, 16), 16)
    turn = lax.rem(y - x + 4, 4)

    def put(j, value):
        wide[...] = value.astype(F32)
        rows = pl.ds(pl.multiple_of(lax.rem(start, 16), 8), 8)
        out[:, pl.ds(pl.multiple_of(lax.rem(y + j, 4) * KB, 128), KB)] = wide[rows, :]

    @pl.when(core == 0)
    def _():
        for j in range(4):
            put(j, block[j, even, :])

    @pl.when(core == 1)
    def _():
        put(0, block[turn, even, :])
        put(1, side1[turn, even, :])
        put(3, side3[turn, even, :])

        @pl.when(turn < 2)
        def _():
            put(2, low[jnp.minimum(turn, 1), even, :])

        @pl.when(turn >= 2)
        def _():
            put(2, high[jnp.maximum(turn - 2, 0), even, :])


def finish_kernel(groups, where, own, oth, labels, bias, *refs):
    actives, ya = refs[:4], refs[4]
    grad, bias_grad, loss, logits, slopes = refs[5:]
    core, x, y = where[0], where[1], where[2]
    lane = lax.broadcasted_iota(jnp.int32, (8, 128), 1)

    def unpack(source, start, parity):
        for d in range(4):
            g = lax.rem(start + d, 4) * 2 + parity
            for i in range(8):
                tile = source[d, :, 128 * i : 128 * (i + 1)]
                logits[g, 8 * i : 8 * i + 8, :] = tile
                logits[g, 64 + 8 * i : 72 + 8 * i, :] = pltpu.roll(tile, 64, 1)

    @pl.when(core == 0)
    def _():
        unpack(own, x, 0)
        unpack(oth, y, 1)

    @pl.when(core == 1)
    def _():
        unpack(oth, x, 0)
        unpack(own, y, 1)

    slopes[...] = jnp.zeros_like(slopes)
    total = jnp.zeros((128, 64), F32)
    sums = jnp.zeros((1, 64), F32)
    for g in range(groups):
        value = logits[g, :, :64] + bias[...]
        target = labels[128 * g : 128 * (g + 1), :].astype(F32)
        slope = (jax.nn.sigmoid(value) - target).astype(BF16)
        slopes[g, :, :64] = slope
        total = total + (jax.nn.softplus(value) - target * value)
        sums = sums + jnp.sum(slope.astype(F32), axis=0, keepdims=True)
    loss[...] = jnp.broadcast_to(
        jnp.sum(jnp.sum(total, axis=1, keepdims=True), axis=0, keepdims=True) / (groups * 128 * 64),
        loss.shape,
    )
    bias_grad[...] = sums / 128

    turned = jnp.zeros((128, ya.shape[2]), F32)
    for d in range(4):
        g = lax.rem(x + d, 4) * 2
        for active, slope in ((actives[d][...], slopes[g]), (ya[d], slopes[g + 1])):
            turned = turned + lax.dot_general(
                slope, active, (((0,), (0,)), ((), ())), preferred_element_type=F32
            )
    grad[...] = (turned / 128)[:64]


def on_device(
    residual, encoder, encoder_bias, thresholds, decoder, decoder_bias, probes, probe_bias, labels
):
    per_group = residual.shape[0]
    lat = encoder.shape[1]
    pos = lax.axis_index(AXES)
    core = pos % 2
    x, z, y = (pos // 2) % 4, (pos // 8) % 4, pos // 32
    is0 = core == 0
    first = jnp.where(is0, x, y)
    second = jnp.where(is0, y, z)
    third = jnp.where(is0, z, x)
    where = jnp.stack([core, x, y, z, first, second, third]).astype(jnp.int32)
    probes2 = jnp.concatenate([probes, probes], axis=1)

    parts = [residual] + [pull(residual, "z", "z", d) for d in (1, 2, 3)]
    unit = absolute(parts, z).transpose(1, 0, 2).reshape(per_group, KB)
    unit, where, probes2, encoder, decoder = lax.optimization_barrier(
        (unit, where, probes2, encoder, decoder)
    )
    unit = settle(unit)
    unit, encoder, decoder = lax.optimization_barrier((unit, encoder, decoder))
    encoder, decoder = load(encoder), load(decoder)
    pulled = [pull(unit, "y", "x", d) for d in (1, 2, 3)]
    unit, pulled, encoder, decoder = lax.optimization_barrier((unit, pulled, encoder, decoder))
    block = collect([unit, *pulled])
    other = swap(block)
    sides = {d: pull(block, "x", "y", d) for d in (1, 3)}

    cut = thresholds[None]
    bias = encoder_bias[None]
    xa = {}

    def run(stage, blocks, acc):
        xa[stage], acc = encode(stage, None, where, blocks, encoder, bias, cut, acc)
        return acc

    acc = run(0, [block, other], None)
    sides, acc = lax.optimization_barrier((sides, acc))
    low, high = halves(sides[1], sides[3])
    far = [pull(low, "x", "y", 1), pull(high, "x", "y", 3)]
    acc = run(1, [sides[1], swap(sides[1])], acc)
    acc = run(3, [sides[3], swap(sides[3])], acc)
    far, acc = lax.optimization_barrier((far, acc))
    mixed = encode(2, 0, where, far, encoder, bias, cut, acc)
    others = [swap(half) for half in far]
    xa[2], acc = encode(2, 1, where, others, encoder, bias, cut, acc, mixed)
    ya = acc.reshape(4, 128, lat)

    keep, got = {}, {}

    def part(d, left):
        keep[d], *send = decode(d, where, left, ya, decoder, probes2)
        got[d] = [swap(half) for half in send]

    part(2, xa[2])
    over = pair_sum(None, keep[2], *got[2])
    over, left1, left3 = lax.optimization_barrier((over, xa[1], xa[3]))
    through = [pull(over[0], "x", "y", 3), pull(over[1], "x", "y", 1)]
    part(1, left1)
    part(3, left3)
    through, keep[1], keep[3], left0 = lax.optimization_barrier(
        (through, keep[1], keep[3], xa[0])
    )
    (message1,) = pair_sum(0, keep[1], *got[1], through[0])
    (message3,) = pair_sum(1, keep[3], *got[3], through[1])
    message1, message3, left0 = lax.optimization_barrier((message1, message3, left0))
    part(0, left0)
    mine = {1: pull(message1, "x", "y", 3), 3: pull(message3, "x", "y", 1)}
    (tokens,) = small_call(
        rows_kernel, "own_rows", [((8, D), F32)],
        where, block, sides[1], *far, sides[3], scratch=[pltpu.VMEM((16, KB), F32)],
    )

    m2 = small_call(
        first_kernel, "first_sum", [((32, W2), BF16)] * 4,
        where, keep[0], *got[0], mine[1], mine[3],
    )
    g2 = [pull(m2[d], "y", "z", 4 - d) for d in (1, 2, 3)]
    m3 = small_call(
        second_kernel, "second_sum", [((8, W3), F32)] * 4, where, m2[0], *g2,
        scratch=[pltpu.VMEM((32, D), F32), pltpu.VMEM((128, 128), F32)],
    )
    g3 = [pull(m3[d], "z", "x", 4 - d) for d in (1, 2, 3)]
    err, packed = small_call(
        third_kernel, "third_sum", [((8, 128), F32), ((8, 1024), F32)],
        m3[0], *g3, tokens, decoder_bias[None], scalars=0,
    )
    owners = []
    for p, c in coords():
        s = (p["x"], p["y"], p["z"]) if c == 0 else (p["y"], p["z"], p["x"])
        owners.append((place(p, c), s[0] * 32 + c * 16 + s[1] * 4 + s[2]))

    pulled = [pull(packed, "x", "y", d) for d in (1, 2, 3)]
    err = lax.ppermute(err, AXES, owners)
    pulled, packed, err = lax.optimization_barrier((pulled, packed, err))
    mine = collect([packed, *pulled])
    theirs = swap(mine)
    error = err[:, 0]
    probe_grad, bias_grad, mean_loss = small_call(
        functools.partial(finish_kernel, 8), "finish",
        [((64, lat), F32), ((1, 64), F32), ((1, 128), F32)],
        where, mine, theirs, labels, probe_bias[None], xa[0], xa[1], xa[2], xa[3], ya,
        scratch=[pltpu.VMEM((8, 128, 128), F32), pltpu.VMEM((8, 128, 128), BF16)],
    )
    return (error, probe_grad.T, bias_grad[0], mean_loss[0, 0])


def solution(mesh):
    in_specs = (
        P("dp", "latent"),
        P(None, ("latent", "dp")),
        P(("latent", "dp")),
        P(("latent", "dp")),
        P(("latent", "dp"), None),
        P(),
        P(("latent", "dp"), None),
        P(),
        P(),
    )
    out_specs = (P(("latent", "dp")), P(("latent", "dp"), None), P(), P())
    return jax.shard_map(
        on_device, mesh=mesh, in_specs=in_specs, out_specs=out_specs, check_vma=False
    )
```

```python
import functools

import jax
import jax.numpy as jnp
from jax import lax
from jax.experimental import pallas as pl
from jax.experimental.pallas import tpu as pltpu
from jax.sharding import PartitionSpec as P

softness = 0.1
levels = 256.0
AXES = ("latent", "dp")
F32 = jnp.float32
BF16 = jnp.bfloat16
KB = 1152
D = 4608
W = D + 128
WR = W + 256
W2 = D + 512
C = D // 2
W3 = D + 1024
VMEM_LIMIT = 8 * 1024 * 1024
LITTLE = pl.CostEstimate(flops=1000000, bytes_accessed=0, transcendentals=0)


def flat(y, z, x, c):
    return ((y * 4 + z) * 4 + x) * 2 + c


def coords():
    for y in range(4):
        for z in range(4):
            for x in range(4):
                for c in range(2):
                    yield {"y": y, "z": z, "x": x}, c


def place(p, c):
    return flat(p["y"], p["z"], p["x"], c)


def pull_perm(axis0, axis1, step):
    pairs = []
    for p, c in coords():
        axis = (axis0, axis1)[c]
        q = dict(p)
        q[axis] = (p[axis] + step) % 4
        pairs.append((place(q, c), place(p, c)))
    return pairs


def pull(value, axis0, axis1, step):
    return lax.ppermute(value, AXES, pull_perm(axis0, axis1, step))


def swap(value):
    pairs = [(place(p, c), place(p, 1 - c)) for p, c in coords()]
    return lax.ppermute(value, AXES, pairs)


def absolute(parts, start):
    twice = jnp.stack(list(parts) * 2)
    return lax.dynamic_slice_in_dim(twice, lax.rem(4 - start, 4), 4, 0)


def load_kernel(source, target, sems):
    pieces = sems.shape[0]
    rows = source.shape[0] // pieces
    copies = []
    for i in range(pieces):
        span = slice(rows * i, rows * (i + 1))
        copies.append(pltpu.make_async_copy(source.at[span], target.at[span], sems.at[i]))
    for copy in copies:
        copy.start()
    for copy in copies:
        copy.wait()


def load(value):
    held = pl.pallas_call(
        load_kernel,
        in_specs=[pl.BlockSpec(memory_space=pltpu.HBM)],
        out_specs=pl.BlockSpec(memory_space=pltpu.VMEM),
        out_shape=jax.ShapeDtypeStruct(value.shape, value.dtype),
        scratch_shapes=[pltpu.SemaphoreType.DMA((4,))],
        compiler_params=pltpu.CompilerParams(vmem_limit_bytes=VMEM_LIMIT),
        cost_estimate=LITTLE,
        name="load",
    )(pltpu.with_memory_space_constraint(value, pltpu.HBM))
    return near(held)


def near(value):
    return pltpu.with_memory_space_constraint(value, pltpu.VMEM)


STAGES = (0, 1, 3, 2)


def encode_kernel(stage, which, tile, where, *refs):
    count = 1 if which is None else 2
    blocks = refs[: 2 * count if which is None else count]
    refs = refs[len(blocks) :]
    enc, bias, cut = refs[:3]
    acc = None if stage == STAGES[0] else refs[3]
    xa, ya = refs[-2:]
    core, y = where[0], where[2]
    depth = 4 // count

    def rows(step):
        return pl.ds(pl.multiple_of(lax.rem(y + step, 4) * KB, KB), KB)

    def activate(preact, cols):
        cutoff = cut[:, cols].astype(F32) / levels
        gate = jax.nn.sigmoid((preact - cutoff) / softness)
        return (preact * gate).astype(BF16)

    def tiles(*works):
        if stage == STAGES[-1]:
            for n in range(enc.shape[1] // tile):
                for work in works:
                    work(slice(tile * n, tile * (n + 1)))
            return

        @pl.loop(0, enc.shape[1] // tile)
        def _(n):
            for work in works:
                work(pl.ds(pl.multiple_of(n * tile, tile), tile))

    def few(parts):
        def work(cols):
            pre = bias[:, cols] + sum(
                jnp.dot(
                    parts[j // depth][j % depth], enc[rows(j), cols], preferred_element_type=F32
                )
                for j in range(4)
            )
            xa[:, cols] = activate(pre, cols)

        return work

    def many(parts):
        def work(cols):
            for i in range(count):
                part = jnp.dot(
                    parts[i][...].reshape(128 * depth, KB),
                    enc[rows(stage), cols],
                    preferred_element_type=F32,
                )
                span = slice(128 * depth * i, 128 * depth * (i + 1))
                if acc is not None:
                    part = part + acc[span, cols]
                if stage == STAGES[-1]:
                    ya[span, cols] = activate(part + bias[:, cols], cols)
                else:
                    ya[span, cols] = part

        return work

    for turn in (0, 1):

        @pl.when(core == turn)
        def _(turn=turn):
            if which is None:
                tiles(few([blocks[turn]]), many([blocks[1 - turn]]))
            elif which == turn:
                tiles(few(blocks))
            else:
                tiles(many(blocks))


def encode(stage, which, where, blocks, enc, bias, cut, acc, done=()):
    lat = enc.shape[1]
    vmem = pl.BlockSpec(memory_space=pltpu.VMEM)
    args = [*blocks, enc, bias, cut]
    aliases = {}
    if acc is not None:
        args.append(acc)
        if stage != STAGES[-1]:
            aliases = {len(args): 1}
    for i, value in enumerate(done):
        args.append(value)
        aliases[len(args)] = i
    return pl.pallas_call(
        functools.partial(encode_kernel, stage, which, 256),
        in_specs=[pl.BlockSpec(memory_space=pltpu.SMEM)] + [vmem] * len(args),
        out_specs=[vmem, vmem],
        out_shape=[
            jax.ShapeDtypeStruct((128, lat), BF16),
            jax.ShapeDtypeStruct((512, lat), BF16 if stage == STAGES[-1] else F32),
        ],
        input_output_aliases=aliases,
        compiler_params=pltpu.CompilerParams(vmem_limit_bytes=VMEM_LIMIT),
        cost_estimate=LITTLE,
        name="encode",
    )(where, *args)


def split(total):
    lane = lax.broadcasted_iota(jnp.int32, total.shape, total.ndim - 1)
    high = total.astype(BF16).astype(F32)
    return jnp.where(lane < 64, high, total - high)


def joined(pair):
    return pair + pltpu.roll(pair, 64, pair.ndim - 1)


def decode_kernel(step, tile, where, xa, ya, dec, probes, keep, send0, send1, lhs):
    core = where[0]
    pick = lax.rem(where[2] + step - where[1] + 4, 4)
    lhs[pl.ds(pl.multiple_of(core * 128, 128), 128), :] = xa[...]
    lhs[pl.ds(pl.multiple_of((1 - core) * 128, 128), 128), :] = ya[pick]
    logits = split(jnp.dot(lhs[...], probes[...], preferred_element_type=F32)).astype(BF16)
    keep[:, D:] = logits[:128]
    send1[:, C:] = logits[128:]

    if step == 0:
        for i, send in enumerate((send0, send1)):

            @pl.loop(0, C // tile)
            def _(n, i=i, send=send):
                cols = pl.ds(pl.multiple_of(C * i + n * tile, tile), tile)
                out = jnp.dot(lhs[...], dec[:, cols], preferred_element_type=F32).astype(BF16)
                keep[:, cols] = out[:128]
                send[:, pl.ds(pl.multiple_of(n * tile, tile), tile)] = out[128:]

        return
    for n in range(D // tile):
        cols = slice(tile * n, tile * (n + 1))
        send, start = (send0, tile * n) if tile * n < C else (send1, tile * n - C)
        out = jnp.dot(lhs[...], dec[:, cols], preferred_element_type=F32).astype(BF16)
        keep[:, cols] = out[:128]
        send[:, start : start + tile] = out[128:]


def decode(step, where, xa, ya, dec, probes):
    lat = dec.shape[0]
    vmem = pl.BlockSpec(memory_space=pltpu.VMEM)
    return pl.pallas_call(
        functools.partial(decode_kernel, step, 768),
        in_specs=[pl.BlockSpec(memory_space=pltpu.SMEM)] + [vmem] * 4,
        out_specs=[vmem] * 3,
        scratch_shapes=[pltpu.VMEM((256, lat), BF16)],
        out_shape=[jax.ShapeDtypeStruct((128, w), BF16) for w in (W, C, W - C)],
        compiler_params=pltpu.CompilerParams(vmem_limit_bytes=VMEM_LIMIT),
        cost_estimate=LITTLE,
        name="decode",
    )(where, xa, ya, dec, probes)


def small_call(kernel, name, outs, *args, scalars=1, scratch=()):
    vmem = pl.BlockSpec(memory_space=pltpu.VMEM)
    smem = pl.BlockSpec(memory_space=pltpu.SMEM)
    return pl.pallas_call(
        kernel,
        in_specs=[smem] * scalars + [vmem] * (len(args) - scalars),
        out_specs=[vmem] * len(outs),
        out_shape=[jax.ShapeDtypeStruct(shape, kind) for shape, kind in outs],
        scratch_shapes=list(scratch),
        compiler_params=pltpu.CompilerParams(vmem_limit_bytes=VMEM_LIMIT),
        cost_estimate=LITTLE,
        name=name,
    )(*args)


def pair_kernel(shift, a, b0, b1, *refs):
    low, high = slice(0, C), slice(C, D)
    outs = refs if shift is None else refs[1:]
    for i in range(2):
        rows = slice(64 * i, 64 * (i + 1))
        out, spot = (outs[i], slice(0, 64)) if shift is None else (outs[0], rows)
        for cols, other in ((low, b0[rows]), (high, b1[rows, :C])):
            part = a[rows, cols].astype(F32) + other.astype(F32)
            if i == shift:
                part = part + refs[0][:, cols].astype(F32)
            out[spot, cols] = part.astype(BF16)
        logits = a[rows, D:].astype(F32) + b1[rows, C:].astype(F32)
        if i == shift:
            logits = logits + refs[0][:, D:W].astype(F32)
        out[spot, D:W] = split(joined(logits)).astype(BF16)
        if shift is None:
            out[:, W:] = jnp.zeros((64, WR - W), BF16)


def pair_sum(shift, *args):
    outs = [((64, WR), BF16)] * 2 if shift is None else [((128, W), BF16)]
    kernel = functools.partial(pair_kernel, shift)
    return small_call(kernel, "pair_sum", outs, *args, scalars=0)


def first_kernel(where, a0, b0, b1, g1, g3, *outs):
    spot = where[5]
    logits = b1[:, C:].astype(F32) + sum(r[:, D:].astype(F32) for r in (a0, g1, g3))
    logits = split(joined(logits)).astype(BF16)
    for d, out in enumerate(outs):
        rows = pl.ds(pl.multiple_of(lax.rem(spot + d, 4) * 32, 32), 32)
        for cols, other in ((slice(0, C), b0[rows, :]), (slice(C, D), b1[rows, :C])):
            part = other.astype(F32) + sum(r[rows, cols].astype(F32) for r in (a0, g1, g3))
            out[:, cols] = part.astype(BF16)
        for k in range(4):
            out[:, D + 128 * k : D + 128 * (k + 1)] = logits[32 * k : 32 * (k + 1)]


def second_kernel(where, m0, g1, g2, g3, *refs):
    outs, total, wide = refs[:4], refs[4], refs[5]
    spot = where[6]

    def four(cols):
        a0, a1, a2, a3 = (r[:, cols].astype(F32) for r in (m0, g1, g2, g3))
        return (a0 + a2) + (a1 + a3)

    total[...] = four(slice(0, D))
    for k in range(4):
        cols = slice(D + 128 * k, D + 128 * (k + 1))
        l0, l1, l2, l3 = (joined(r[:, cols].astype(F32)) for r in (m0, g1, g2, g3))
        wide[32 * k : 32 * (k + 1), :] = (l0 + l2) + (l1 + l3)
    lane = lax.broadcasted_iota(jnp.int32, (8, 128), 1)
    packed = [
        jnp.where(lane < 64, wide[8 * i : 8 * i + 8, :], wide[64 + 8 * i : 72 + 8 * i, :])
        for i in range(8)
    ]
    for d, out in enumerate(outs):
        rows = pl.ds(pl.multiple_of(lax.rem(spot + d, 4) * 8, 8), 8)
        out[:, :D] = total[rows, :]
        for i in range(8):
            out[:, D + 128 * i : D + 128 * (i + 1)] = packed[i]


def third_kernel(m0, g1, g2, g3, tokens, bias, err, logits):
    def four(cols):
        a0, a1, a2, a3 = (r[:, cols] for r in (m0, g1, g2, g3))
        return (a0 + a2) + (a1 + a3)

    gap = tokens[...] - (four(slice(0, D)) + bias[...])
    err[...] = jnp.broadcast_to(jnp.sum(gap * gap, axis=1, keepdims=True) / D, err.shape)
    logits[...] = four(slice(D, W3))


def collect_kernel(*refs):
    for i, ref in enumerate(refs[:4]):
        refs[4][i] = ref[...]


def collect(parts):
    shape = (4, *parts[0].shape)
    return small_call(collect_kernel, "collect", [(shape, parts[0].dtype)], *parts, scalars=0)[0]


def settle_kernel(source, target):
    target[...] = source[...]


def settle(value):
    outs = [(value.shape, value.dtype)]
    return small_call(settle_kernel, "settle", outs, value, scalars=0)[0]


def halves_kernel(a, b, low, high):
    low[...] = a[:2]
    high[...] = b[2:]


def halves(a, b):
    shape = (2, *a.shape[1:])
    outs = [(shape, a.dtype)] * 2
    return small_call(halves_kernel, "halves", outs, a, b, scalars=0)


def rows_kernel(where, block, side1, low, high, side3, out, wide):
    core, x, y = where[0], where[1], where[2]
    start = where[5] * 32 + where[6] * 8
    even = pl.ds(pl.multiple_of(start // 16 * 16, 16), 16)
    turn = lax.rem(y - x + 4, 4)

    def put(j, value):
        wide[...] = value.astype(F32)
        rows = pl.ds(pl.multiple_of(lax.rem(start, 16), 8), 8)
        out[:, pl.ds(pl.multiple_of(lax.rem(y + j, 4) * KB, 128), KB)] = wide[rows, :]

    @pl.when(core == 0)
    def _():
        for j in range(4):
            put(j, block[j, even, :])

    @pl.when(core == 1)
    def _():
        put(0, block[turn, even, :])
        put(1, side1[turn, even, :])
        put(3, side3[turn, even, :])

        @pl.when(turn < 2)
        def _():
            put(2, low[jnp.minimum(turn, 1), even, :])

        @pl.when(turn >= 2)
        def _():
            put(2, high[jnp.maximum(turn - 2, 0), even, :])


def finish_kernel(groups, where, own, oth, labels, bias, *refs):
    actives, ya = refs[:4], refs[4]
    grad, bias_grad, loss, logits, slopes = refs[5:]
    core, x, y = where[0], where[1], where[2]
    lane = lax.broadcasted_iota(jnp.int32, (8, 128), 1)

    def unpack(source, start, parity):
        for d in range(4):
            g = lax.rem(start + d, 4) * 2 + parity
            for i in range(8):
                tile = source[d, :, 128 * i : 128 * (i + 1)]
                logits[g, 8 * i : 8 * i + 8, :] = tile
                logits[g, 64 + 8 * i : 72 + 8 * i, :] = pltpu.roll(tile, 64, 1)

    @pl.when(core == 0)
    def _():
        unpack(own, x, 0)
        unpack(oth, y, 1)

    @pl.when(core == 1)
    def _():
        unpack(oth, x, 0)
        unpack(own, y, 1)

    slopes[...] = jnp.zeros_like(slopes)
    total = jnp.zeros((128, 64), F32)
    sums = jnp.zeros((1, 64), F32)
    for g in range(groups):
        value = logits[g, :, :64] + bias[...]
        target = labels[128 * g : 128 * (g + 1), :].astype(F32)
        slope = (jax.nn.sigmoid(value) - target).astype(BF16)
        slopes[g, :, :64] = slope
        total = total + (jax.nn.softplus(value) - target * value)
        sums = sums + jnp.sum(slope.astype(F32), axis=0, keepdims=True)
    loss[...] = jnp.broadcast_to(
        jnp.sum(jnp.sum(total, axis=1, keepdims=True), axis=0, keepdims=True) / (groups * 128 * 64),
        loss.shape,
    )
    bias_grad[...] = sums / 128

    turned = jnp.zeros((128, ya.shape[2]), F32)
    for d in range(4):
        g = lax.rem(x + d, 4) * 2
        for active, slope in ((actives[d][...], slopes[g]), (ya[d], slopes[g + 1])):
            turned = turned + lax.dot_general(
                slope, active, (((0,), (0,)), ((), ())), preferred_element_type=F32
            )
    grad[...] = (turned / 128)[:64]


def on_device(
    residual, encoder, encoder_bias, thresholds, decoder, decoder_bias, probes, probe_bias, labels
):
    per_group = residual.shape[0]
    lat = encoder.shape[1]
    pos = lax.axis_index(AXES)
    core = pos % 2
    x, z, y = (pos // 2) % 4, (pos // 8) % 4, pos // 32
    is0 = core == 0
    first = jnp.where(is0, x, y)
    second = jnp.where(is0, y, z)
    third = jnp.where(is0, z, x)
    where = jnp.stack([core, x, y, z, first, second, third]).astype(jnp.int32)
    probes2 = jnp.concatenate([probes, probes], axis=1)

    parts = [residual] + [pull(residual, "z", "z", d) for d in (1, 2, 3)]
    unit = absolute(parts, z).transpose(1, 0, 2).reshape(per_group, KB)
    unit, where, probes2, encoder, decoder = lax.optimization_barrier(
        (unit, where, probes2, encoder, decoder)
    )
    unit = settle(unit)
    unit, encoder, decoder = lax.optimization_barrier((unit, encoder, decoder))
    encoder, decoder = load(encoder), load(decoder)
    pulled = [pull(unit, "y", "x", d) for d in (1, 2, 3)]
    unit, pulled, encoder, decoder = lax.optimization_barrier((unit, pulled, encoder, decoder))
    block = collect([unit, *pulled])
    other = swap(block)
    sides = {d: pull(block, "x", "y", d) for d in (1, 3)}

    cut = thresholds[None]
    bias = encoder_bias[None]
    xa = {}

    def run(stage, blocks, acc):
        xa[stage], acc = encode(stage, None, where, blocks, encoder, bias, cut, acc)
        return acc

    acc = run(0, [block, other], None)
    sides, acc = lax.optimization_barrier((sides, acc))
    low, high = halves(sides[1], sides[3])
    far = [pull(low, "x", "y", 1), pull(high, "x", "y", 3)]
    acc = run(1, [sides[1], swap(sides[1])], acc)
    acc = run(3, [sides[3], swap(sides[3])], acc)
    far, acc = lax.optimization_barrier((far, acc))
    mixed = encode(2, 0, where, far, encoder, bias, cut, acc)
    others = [swap(half) for half in far]
    xa[2], acc = encode(2, 1, where, others, encoder, bias, cut, acc, mixed)
    ya = acc.reshape(4, 128, lat)

    keep, got = {}, {}

    def part(d, left):
        keep[d], *send = decode(d, where, left, ya, decoder, probes2)
        got[d] = [swap(half) for half in send]

    part(2, xa[2])
    over = pair_sum(None, keep[2], *got[2])
    over, left1, left3 = lax.optimization_barrier((over, xa[1], xa[3]))
    through = [pull(over[0], "x", "y", 3), pull(over[1], "x", "y", 1)]
    part(1, left1)
    part(3, left3)
    through, keep[1], keep[3], left0 = lax.optimization_barrier(
        (through, keep[1], keep[3], xa[0])
    )
    (message1,) = pair_sum(0, keep[1], *got[1], through[0])
    (message3,) = pair_sum(1, keep[3], *got[3], through[1])
    message1, message3, left0 = lax.optimization_barrier((message1, message3, left0))
    part(0, left0)
    mine = {1: pull(message1, "x", "y", 3), 3: pull(message3, "x", "y", 1)}
    (tokens,) = small_call(
        rows_kernel, "own_rows", [((8, D), F32)],
        where, block, sides[1], *far, sides[3], scratch=[pltpu.VMEM((16, KB), F32)],
    )

    m2 = small_call(
        first_kernel, "first_sum", [((32, W2), BF16)] * 4,
        where, keep[0], *got[0], mine[1], mine[3],
    )
    g2 = [pull(m2[d], "y", "z", 4 - d) for d in (1, 2, 3)]
    m3 = small_call(
        second_kernel, "second_sum", [((8, W3), F32)] * 4, where, m2[0], *g2,
        scratch=[pltpu.VMEM((32, D), F32), pltpu.VMEM((128, 128), F32)],
    )
    g3 = [pull(m3[d], "z", "x", 4 - d) for d in (1, 2, 3)]
    err, packed = small_call(
        third_kernel, "third_sum", [((8, 128), F32), ((8, 1024), F32)],
        m3[0], *g3, tokens, decoder_bias[None], scalars=0,
    )
    owners = []
    for p, c in coords():
        s = (p["x"], p["y"], p["z"]) if c == 0 else (p["y"], p["z"], p["x"])
        owners.append((place(p, c), s[0] * 32 + c * 16 + s[1] * 4 + s[2]))

    pulled = [pull(packed, "x", "y", d) for d in (1, 2, 3)]
    err = lax.ppermute(err, AXES, owners)
    pulled, packed, err = lax.optimization_barrier((pulled, packed, err))
    mine = collect([packed, *pulled])
    theirs = swap(mine)
    error = err[:, 0]
    probe_grad, bias_grad, mean_loss = small_call(
        functools.partial(finish_kernel, 8), "finish",
        [((64, lat), F32), ((1, 64), F32), ((1, 128), F32)],
        where, mine, theirs, labels, probe_bias[None], xa[0], xa[1], xa[2], xa[3], ya,
        scratch=[pltpu.VMEM((8, 128, 128), F32), pltpu.VMEM((8, 128, 128), BF16)],
    )
    return (error, probe_grad.T, bias_grad[0], mean_loss[0, 0])


def solution(mesh):
    in_specs = (
        P("dp", "latent"),
        P(None, ("latent", "dp")),
        P(("latent", "dp")),
        P(("latent", "dp")),
        P(("latent", "dp"), None),
        P(),
        P(("latent", "dp"), None),
        P(),
        P(),
    )
    out_specs = (P(("latent", "dp")), P(("latent", "dp"), None), P(), P())
    return jax.shard_map(
        on_device, mesh=mesh, in_specs=in_specs, out_specs=out_specs, check_vma=False
    )
```

```python
import functools

import jax
import jax.numpy as jnp
from jax import lax
from jax.experimental import pallas as pl
from jax.experimental.pallas import tpu as pltpu
from jax.sharding import PartitionSpec as P

softness = 0.1
levels = 256.0
AXES = ("latent", "dp")
F32 = jnp.float32
BF16 = jnp.bfloat16
KB = 1152
D = 4608
W = D + 128
WR = W + 256
W2 = D + 512
C = D // 2
W3 = D + 1024
VMEM_LIMIT = 8 * 1024 * 1024
LITTLE = pl.CostEstimate(flops=1000000, bytes_accessed=0, transcendentals=0)


def flat(y, z, x, c):
    return ((y * 4 + z) * 4 + x) * 2 + c


def coords():
    for y in range(4):
        for z in range(4):
            for x in range(4):
                for c in range(2):
                    yield {"y": y, "z": z, "x": x}, c


def place(p, c):
    return flat(p["y"], p["z"], p["x"], c)


def pull_perm(axis0, axis1, step):
    pairs = []
    for p, c in coords():
        axis = (axis0, axis1)[c]
        q = dict(p)
        q[axis] = (p[axis] + step) % 4
        pairs.append((place(q, c), place(p, c)))
    return pairs


def pull(value, axis0, axis1, step):
    return lax.ppermute(value, AXES, pull_perm(axis0, axis1, step))


def swap(value):
    pairs = [(place(p, c), place(p, 1 - c)) for p, c in coords()]
    return lax.ppermute(value, AXES, pairs)


def absolute(parts, start):
    twice = jnp.stack(list(parts) * 2)
    return lax.dynamic_slice_in_dim(twice, lax.rem(4 - start, 4), 4, 0)


def load_kernel(source, target, sems):
    pieces = sems.shape[0]
    rows = source.shape[0] // pieces
    copies = []
    for i in range(pieces):
        span = slice(rows * i, rows * (i + 1))
        copies.append(pltpu.make_async_copy(source.at[span], target.at[span], sems.at[i]))
    for copy in copies:
        copy.start()
    for copy in copies:
        copy.wait()


def load(value):
    held = pl.pallas_call(
        load_kernel,
        in_specs=[pl.BlockSpec(memory_space=pltpu.HBM)],
        out_specs=pl.BlockSpec(memory_space=pltpu.VMEM),
        out_shape=jax.ShapeDtypeStruct(value.shape, value.dtype),
        scratch_shapes=[pltpu.SemaphoreType.DMA((4,))],
        compiler_params=pltpu.CompilerParams(vmem_limit_bytes=VMEM_LIMIT),
        cost_estimate=LITTLE,
        name="load",
    )(pltpu.with_memory_space_constraint(value, pltpu.HBM))
    return near(held)


def near(value):
    return pltpu.with_memory_space_constraint(value, pltpu.VMEM)


STAGES = (0, 1, 3, 2)


def encode_kernel(stage, which, tile, where, *refs):
    count = 1 if which is None else 2
    blocks = refs[: 2 * count if which is None else count]
    refs = refs[len(blocks) :]
    enc, bias, cut = refs[:3]
    acc = None if stage == STAGES[0] else refs[3]
    xa, ya = refs[-2:]
    core, y = where[0], where[2]
    depth = 4 // count

    def rows(step):
        return pl.ds(pl.multiple_of(lax.rem(y + step, 4) * KB, KB), KB)

    def activate(preact, cols):
        cutoff = cut[:, cols].astype(F32) / levels
        gate = jax.nn.sigmoid((preact - cutoff) / softness)
        return (preact * gate).astype(BF16)

    def tiles(*works):
        if stage == STAGES[-1]:
            for n in range(enc.shape[1] // tile):
                for work in works:
                    work(slice(tile * n, tile * (n + 1)))
            return

        @pl.loop(0, enc.shape[1] // tile)
        def _(n):
            for work in works:
                work(pl.ds(pl.multiple_of(n * tile, tile), tile))

    def few(parts):
        def work(cols):
            pre = bias[:, cols] + sum(
                jnp.dot(
                    parts[j // depth][j % depth], enc[rows(j), cols], preferred_element_type=F32
                )
                for j in range(4)
            )
            xa[:, cols] = activate(pre, cols)

        return work

    def many(parts):
        def work(cols):
            for i in range(count):
                part = jnp.dot(
                    parts[i][...].reshape(128 * depth, KB),
                    enc[rows(stage), cols],
                    preferred_element_type=F32,
                )
                span = slice(128 * depth * i, 128 * depth * (i + 1))
                if acc is not None:
                    part = part + acc[span, cols]
                if stage == STAGES[-1]:
                    ya[span, cols] = activate(part + bias[:, cols], cols)
                else:
                    ya[span, cols] = part

        return work

    for turn in (0, 1):

        @pl.when(core == turn)
        def _(turn=turn):
            if which is None:
                tiles(few([blocks[turn]]), many([blocks[1 - turn]]))
            elif which == turn:
                tiles(few(blocks))
            else:
                tiles(many(blocks))


def encode(stage, which, where, blocks, enc, bias, cut, acc, done=()):
    lat = enc.shape[1]
    vmem = pl.BlockSpec(memory_space=pltpu.VMEM)
    args = [*blocks, enc, bias, cut]
    aliases = {}
    if acc is not None:
        args.append(acc)
        if stage != STAGES[-1]:
            aliases = {len(args): 1}
    for i, value in enumerate(done):
        args.append(value)
        aliases[len(args)] = i
    return pl.pallas_call(
        functools.partial(encode_kernel, stage, which, 256),
        in_specs=[pl.BlockSpec(memory_space=pltpu.SMEM)] + [vmem] * len(args),
        out_specs=[vmem, vmem],
        out_shape=[
            jax.ShapeDtypeStruct((128, lat), BF16),
            jax.ShapeDtypeStruct((512, lat), BF16 if stage == STAGES[-1] else F32),
        ],
        input_output_aliases=aliases,
        compiler_params=pltpu.CompilerParams(vmem_limit_bytes=VMEM_LIMIT),
        cost_estimate=LITTLE,
        name="encode",
    )(where, *args)


def split(total):
    lane = lax.broadcasted_iota(jnp.int32, total.shape, total.ndim - 1)
    high = total.astype(BF16).astype(F32)
    return jnp.where(lane < 64, high, total - high)


def joined(pair):
    return pair + pltpu.roll(pair, 64, pair.ndim - 1)


def decode_kernel(step, tile, where, xa, ya, dec, probes, keep, send0, send1, lhs):
    core = where[0]
    pick = lax.rem(where[2] + step - where[1] + 4, 4)
    lhs[pl.ds(pl.multiple_of(core * 128, 128), 128), :] = xa[...]
    lhs[pl.ds(pl.multiple_of((1 - core) * 128, 128), 128), :] = ya[pick]
    logits = split(jnp.dot(lhs[...], probes[...], preferred_element_type=F32)).astype(BF16)
    keep[:, D:] = logits[:128]
    send1[:, C:] = logits[128:]

    if step == 0:
        for i, send in enumerate((send0, send1)):

            @pl.loop(0, C // tile)
            def _(n, i=i, send=send):
                cols = pl.ds(pl.multiple_of(C * i + n * tile, tile), tile)
                out = jnp.dot(lhs[...], dec[:, cols], preferred_element_type=F32).astype(BF16)
                keep[:, cols] = out[:128]
                send[:, pl.ds(pl.multiple_of(n * tile, tile), tile)] = out[128:]

        return
    for n in range(D // tile):
        cols = slice(tile * n, tile * (n + 1))
        send, start = (send0, tile * n) if tile * n < C else (send1, tile * n - C)
        out = jnp.dot(lhs[...], dec[:, cols], preferred_element_type=F32).astype(BF16)
        keep[:, cols] = out[:128]
        send[:, start : start + tile] = out[128:]


def decode(step, where, xa, ya, dec, probes):
    lat = dec.shape[0]
    vmem = pl.BlockSpec(memory_space=pltpu.VMEM)
    return pl.pallas_call(
        functools.partial(decode_kernel, step, 768),
        in_specs=[pl.BlockSpec(memory_space=pltpu.SMEM)] + [vmem] * 4,
        out_specs=[vmem] * 3,
        scratch_shapes=[pltpu.VMEM((256, lat), BF16)],
        out_shape=[jax.ShapeDtypeStruct((128, w), BF16) for w in (W, C, W - C)],
        compiler_params=pltpu.CompilerParams(vmem_limit_bytes=VMEM_LIMIT),
        cost_estimate=LITTLE,
        name="decode",
    )(where, xa, ya, dec, probes)


def small_call(kernel, name, outs, *args, scalars=1, scratch=()):
    vmem = pl.BlockSpec(memory_space=pltpu.VMEM)
    smem = pl.BlockSpec(memory_space=pltpu.SMEM)
    return pl.pallas_call(
        kernel,
        in_specs=[smem] * scalars + [vmem] * (len(args) - scalars),
        out_specs=[vmem] * len(outs),
        out_shape=[jax.ShapeDtypeStruct(shape, kind) for shape, kind in outs],
        scratch_shapes=list(scratch),
        compiler_params=pltpu.CompilerParams(vmem_limit_bytes=VMEM_LIMIT),
        cost_estimate=LITTLE,
        name=name,
    )(*args)


def pair_kernel(shift, a, b0, b1, *refs):
    low, high = slice(0, C), slice(C, D)
    outs = refs if shift is None else refs[1:]
    for i in range(2):
        rows = slice(64 * i, 64 * (i + 1))
        out, spot = (outs[i], slice(0, 64)) if shift is None else (outs[0], rows)
        for cols, other in ((low, b0[rows]), (high, b1[rows, :C])):
            part = a[rows, cols].astype(F32) + other.astype(F32)
            if i == shift:
                part = part + refs[0][:, cols].astype(F32)
            out[spot, cols] = part.astype(BF16)
        logits = a[rows, D:].astype(F32) + b1[rows, C:].astype(F32)
        if i == shift:
            logits = logits + refs[0][:, D:W].astype(F32)
        out[spot, D:W] = split(joined(logits)).astype(BF16)
        if shift is None:
            out[:, W:] = jnp.zeros((64, WR - W), BF16)


def pair_sum(shift, *args):
    outs = [((64, WR), BF16)] * 2 if shift is None else [((128, W), BF16)]
    kernel = functools.partial(pair_kernel, shift)
    return small_call(kernel, "pair_sum", outs, *args, scalars=0)


def first_kernel(where, a0, b0, b1, g1, g3, *outs):
    spot = where[5]
    logits = b1[:, C:].astype(F32) + sum(r[:, D:].astype(F32) for r in (a0, g1, g3))
    logits = split(joined(logits)).astype(BF16)
    for d, out in enumerate(outs):
        rows = pl.ds(pl.multiple_of(lax.rem(spot + d, 4) * 32, 32), 32)
        for cols, other in ((slice(0, C), b0[rows, :]), (slice(C, D), b1[rows, :C])):
            part = other.astype(F32) + sum(r[rows, cols].astype(F32) for r in (a0, g1, g3))
            out[:, cols] = part.astype(BF16)
        for k in range(4):
            out[:, D + 128 * k : D + 128 * (k + 1)] = logits[32 * k : 32 * (k + 1)]


def second_kernel(where, m0, g1, g2, g3, *refs):
    outs, total, wide = refs[:4], refs[4], refs[5]
    spot = where[6]

    def four(cols):
        a0, a1, a2, a3 = (r[:, cols].astype(F32) for r in (m0, g1, g2, g3))
        return (a0 + a2) + (a1 + a3)

    total[...] = four(slice(0, D))
    for k in range(4):
        cols = slice(D + 128 * k, D + 128 * (k + 1))
        l0, l1, l2, l3 = (joined(r[:, cols].astype(F32)) for r in (m0, g1, g2, g3))
        wide[32 * k : 32 * (k + 1), :] = (l0 + l2) + (l1 + l3)
    lane = lax.broadcasted_iota(jnp.int32, (8, 128), 1)
    packed = [
        jnp.where(lane < 64, wide[8 * i : 8 * i + 8, :], wide[64 + 8 * i : 72 + 8 * i, :])
        for i in range(8)
    ]
    for d, out in enumerate(outs):
        rows = pl.ds(pl.multiple_of(lax.rem(spot + d, 4) * 8, 8), 8)
        out[:, :D] = total[rows, :]
        for i in range(8):
            out[:, D + 128 * i : D + 128 * (i + 1)] = packed[i]


def third_kernel(m0, g1, g2, g3, tokens, bias, err, logits):
    def four(cols):
        a0, a1, a2, a3 = (r[:, cols] for r in (m0, g1, g2, g3))
        return (a0 + a2) + (a1 + a3)

    gap = tokens[...] - (four(slice(0, D)) + bias[...])
    err[...] = jnp.broadcast_to(jnp.sum(gap * gap, axis=1, keepdims=True) / D, err.shape)
    logits[...] = four(slice(D, W3))


def collect_kernel(*refs):
    for i, ref in enumerate(refs[:4]):
        refs[4][i] = ref[...]


def collect(parts):
    shape = (4, *parts[0].shape)
    return small_call(collect_kernel, "collect", [(shape, parts[0].dtype)], *parts, scalars=0)[0]


def settle_kernel(source, target):
    target[...] = source[...]


def settle(value):
    outs = [(value.shape, value.dtype)]
    return small_call(settle_kernel, "settle", outs, value, scalars=0)[0]


def halves_kernel(a, b, low, high):
    low[...] = a[:2]
    high[...] = b[2:]


def halves(a, b):
    shape = (2, *a.shape[1:])
    outs = [(shape, a.dtype)] * 2
    return small_call(halves_kernel, "halves", outs, a, b, scalars=0)


def rows_kernel(where, block, side1, low, high, side3, out, wide):
    core, x, y = where[0], where[1], where[2]
    start = where[5] * 32 + where[6] * 8
    even = pl.ds(pl.multiple_of(start // 16 * 16, 16), 16)
    turn = lax.rem(y - x + 4, 4)

    def put(j, value):
        wide[...] = value.astype(F32)
        rows = pl.ds(pl.multiple_of(lax.rem(start, 16), 8), 8)
        out[:, pl.ds(pl.multiple_of(lax.rem(y + j, 4) * KB, 128), KB)] = wide[rows, :]

    @pl.when(core == 0)
    def _():
        for j in range(4):
            put(j, block[j, even, :])

    @pl.when(core == 1)
    def _():
        put(0, block[turn, even, :])
        put(1, side1[turn, even, :])
        put(3, side3[turn, even, :])

        @pl.when(turn < 2)
        def _():
            put(2, low[jnp.minimum(turn, 1), even, :])

        @pl.when(turn >= 2)
        def _():
            put(2, high[jnp.maximum(turn - 2, 0), even, :])


def finish_kernel(groups, where, own, oth, labels, bias, *refs):
    actives, ya = refs[:4], refs[4]
    grad, bias_grad, loss, logits, slopes = refs[5:]
    core, x, y = where[0], where[1], where[2]
    lane = lax.broadcasted_iota(jnp.int32, (8, 128), 1)

    def unpack(source, start, parity):
        for d in range(4):
            g = lax.rem(start + d, 4) * 2 + parity
            for i in range(8):
                tile = source[d, :, 128 * i : 128 * (i + 1)]
                logits[g, 8 * i : 8 * i + 8, :] = tile
                logits[g, 64 + 8 * i : 72 + 8 * i, :] = pltpu.roll(tile, 64, 1)

    @pl.when(core == 0)
    def _():
        unpack(own, x, 0)
        unpack(oth, y, 1)

    @pl.when(core == 1)
    def _():
        unpack(oth, x, 0)
        unpack(own, y, 1)

    slopes[...] = jnp.zeros_like(slopes)
    total = jnp.zeros((128, 64), F32)
    sums = jnp.zeros((1, 64), F32)
    for g in range(groups):
        value = logits[g, :, :64] + bias[...]
        target = labels[128 * g : 128 * (g + 1), :].astype(F32)
        slope = (jax.nn.sigmoid(value) - target).astype(BF16)
        slopes[g, :, :64] = slope
        total = total + (jax.nn.softplus(value) - target * value)
        sums = sums + jnp.sum(slope.astype(F32), axis=0, keepdims=True)
    loss[...] = jnp.broadcast_to(
        jnp.sum(jnp.sum(total, axis=1, keepdims=True), axis=0, keepdims=True) / (groups * 128 * 64),
        loss.shape,
    )
    bias_grad[...] = sums / 128

    turned = jnp.zeros((128, ya.shape[2]), F32)
    for d in range(4):
        g = lax.rem(x + d, 4) * 2
        for active, slope in ((actives[d][...], slopes[g]), (ya[d], slopes[g + 1])):
            turned = turned + lax.dot_general(
                slope, active, (((0,), (0,)), ((), ())), preferred_element_type=F32
            )
    grad[...] = (turned / 128)[:64]


def on_device(
    residual, encoder, encoder_bias, thresholds, decoder, decoder_bias, probes, probe_bias, labels
):
    per_group = residual.shape[0]
    lat = encoder.shape[1]
    pos = lax.axis_index(AXES)
    core = pos % 2
    x, z, y = (pos // 2) % 4, (pos // 8) % 4, pos // 32
    is0 = core == 0
    first = jnp.where(is0, x, y)
    second = jnp.where(is0, y, z)
    third = jnp.where(is0, z, x)
    where = jnp.stack([core, x, y, z, first, second, third]).astype(jnp.int32)
    probes2 = jnp.concatenate([probes, probes], axis=1)

    parts = [residual] + [pull(residual, "z", "z", d) for d in (1, 2, 3)]
    unit = absolute(parts, z).transpose(1, 0, 2).reshape(per_group, KB)
    unit, where, probes2, encoder, decoder = lax.optimization_barrier(
        (unit, where, probes2, encoder, decoder)
    )
    unit = settle(unit)
    unit, encoder, decoder = lax.optimization_barrier((unit, encoder, decoder))
    encoder, decoder = load(encoder), load(decoder)
    pulled = [pull(unit, "y", "x", d) for d in (1, 2, 3)]
    unit, pulled, encoder, decoder = lax.optimization_barrier((unit, pulled, encoder, decoder))
    block = collect([unit, *pulled])
    other = swap(block)
    sides = {d: pull(block, "x", "y", d) for d in (1, 3)}

    cut = thresholds[None]
    bias = encoder_bias[None]
    xa = {}

    def run(stage, blocks, acc):
        xa[stage], acc = encode(stage, None, where, blocks, encoder, bias, cut, acc)
        return acc

    acc = run(0, [block, other], None)
    sides, acc = lax.optimization_barrier((sides, acc))
    low, high = halves(sides[1], sides[3])
    far = [pull(low, "x", "y", 1), pull(high, "x", "y", 3)]
    acc = run(1, [sides[1], swap(sides[1])], acc)
    acc = run(3, [sides[3], swap(sides[3])], acc)
    far, acc = lax.optimization_barrier((far, acc))
    mixed = encode(2, 0, where, far, encoder, bias, cut, acc)
    others = [swap(half) for half in far]
    xa[2], acc = encode(2, 1, where, others, encoder, bias, cut, acc, mixed)
    ya = acc.reshape(4, 128, lat)

    keep, got = {}, {}

    def part(d, left):
        keep[d], *send = decode(d, where, left, ya, decoder, probes2)
        got[d] = [swap(half) for half in send]

    part(2, xa[2])
    over = pair_sum(None, keep[2], *got[2])
    over, left1, left3 = lax.optimization_barrier((over, xa[1], xa[3]))
    through = [pull(over[0], "x", "y", 3), pull(over[1], "x", "y", 1)]
    part(1, left1)
    part(3, left3)
    through, keep[1], keep[3], left0 = lax.optimization_barrier(
        (through, keep[1], keep[3], xa[0])
    )
    (message1,) = pair_sum(0, keep[1], *got[1], through[0])
    (message3,) = pair_sum(1, keep[3], *got[3], through[1])
    message1, message3, left0 = lax.optimization_barrier((message1, message3, left0))
    part(0, left0)
    mine = {1: pull(message1, "x", "y", 3), 3: pull(message3, "x", "y", 1)}
    (tokens,) = small_call(
        rows_kernel, "own_rows", [((8, D), F32)],
        where, block, sides[1], *far, sides[3], scratch=[pltpu.VMEM((16, KB), F32)],
    )

    m2 = small_call(
        first_kernel, "first_sum", [((32, W2), BF16)] * 4,
        where, keep[0], *got[0], mine[1], mine[3],
    )
    g2 = [pull(m2[d], "y", "z", 4 - d) for d in (1, 2, 3)]
    m3 = small_call(
        second_kernel, "second_sum", [((8, W3), F32)] * 4, where, m2[0], *g2,
        scratch=[pltpu.VMEM((32, D), F32), pltpu.VMEM((128, 128), F32)],
    )
    g3 = [pull(m3[d], "z", "x", 4 - d) for d in (1, 2, 3)]
    err, packed = small_call(
        third_kernel, "third_sum", [((8, 128), F32), ((8, 1024), F32)],
        m3[0], *g3, tokens, decoder_bias[None], scalars=0,
    )
    owners = []
    for p, c in coords():
        s = (p["x"], p["y"], p["z"]) if c == 0 else (p["y"], p["z"], p["x"])
        owners.append((place(p, c), s[0] * 32 + c * 16 + s[1] * 4 + s[2]))

    pulled = [pull(packed, "x", "y", d) for d in (1, 2, 3)]
    mine = collect([packed, *pulled])
    theirs = swap(mine)
    err = lax.ppermute(err, AXES, owners)
    probe_grad, bias_grad, mean_loss = small_call(
        functools.partial(finish_kernel, 8), "finish",
        [((64, lat), F32), ((1, 64), F32), ((1, 128), F32)],
        where, mine, theirs, labels, probe_bias[None], xa[0], xa[1], xa[2], xa[3], ya,
        scratch=[pltpu.VMEM((8, 128, 128), F32), pltpu.VMEM((8, 128, 128), BF16)],
    )
    err, mean_loss = lax.optimization_barrier((err, mean_loss))
    return (err[:, 0], probe_grad.T, bias_grad[0], mean_loss[0, 0])


def solution(mesh):
    in_specs = (
        P("dp", "latent"),
        P(None, ("latent", "dp")),
        P(("latent", "dp")),
        P(("latent", "dp")),
        P(("latent", "dp"), None),
        P(),
        P(("latent", "dp"), None),
        P(),
        P(),
    )
    out_specs = (P(("latent", "dp")), P(("latent", "dp"), None), P(), P())
    return jax.shard_map(
        on_device, mesh=mesh, in_specs=in_specs, out_specs=out_specs, check_vma=False
    )
```

```python
import functools

import jax
import jax.numpy as jnp
from jax import lax
from jax.experimental import pallas as pl
from jax.experimental.pallas import tpu as pltpu
from jax.sharding import PartitionSpec as P

softness = 0.1
levels = 256.0
AXES = ("latent", "dp")
F32 = jnp.float32
BF16 = jnp.bfloat16
KB = 1152
D = 4608
W = D + 128
WR = W + 256
W2 = D + 512
C = D // 2
W3 = D + 1024
VMEM_LIMIT = 8 * 1024 * 1024
LITTLE = pl.CostEstimate(flops=1000000, bytes_accessed=0, transcendentals=0)


def flat(y, z, x, c):
    return ((y * 4 + z) * 4 + x) * 2 + c


def coords():
    for y in range(4):
        for z in range(4):
            for x in range(4):
                for c in range(2):
                    yield {"y": y, "z": z, "x": x}, c


def place(p, c):
    return flat(p["y"], p["z"], p["x"], c)


def pull_perm(axis0, axis1, step):
    pairs = []
    for p, c in coords():
        axis = (axis0, axis1)[c]
        q = dict(p)
        q[axis] = (p[axis] + step) % 4
        pairs.append((place(q, c), place(p, c)))
    return pairs


def pull(value, axis0, axis1, step):
    return lax.ppermute(value, AXES, pull_perm(axis0, axis1, step))


def swap(value):
    pairs = [(place(p, c), place(p, 1 - c)) for p, c in coords()]
    return lax.ppermute(value, AXES, pairs)


def absolute(parts, start):
    twice = jnp.stack(list(parts) * 2)
    return lax.dynamic_slice_in_dim(twice, lax.rem(4 - start, 4), 4, 0)


def load_kernel(source, target, sems):
    pieces = sems.shape[0]
    rows = source.shape[0] // pieces
    copies = []
    for i in range(pieces):
        span = slice(rows * i, rows * (i + 1))
        copies.append(pltpu.make_async_copy(source.at[span], target.at[span], sems.at[i]))
    for copy in copies:
        copy.start()
    for copy in copies:
        copy.wait()


def load(value):
    held = pl.pallas_call(
        load_kernel,
        in_specs=[pl.BlockSpec(memory_space=pltpu.HBM)],
        out_specs=pl.BlockSpec(memory_space=pltpu.VMEM),
        out_shape=jax.ShapeDtypeStruct(value.shape, value.dtype),
        scratch_shapes=[pltpu.SemaphoreType.DMA((4,))],
        compiler_params=pltpu.CompilerParams(vmem_limit_bytes=VMEM_LIMIT),
        cost_estimate=LITTLE,
        name="load",
    )(pltpu.with_memory_space_constraint(value, pltpu.HBM))
    return near(held)


def near(value):
    return pltpu.with_memory_space_constraint(value, pltpu.VMEM)


STAGES = (0, 1, 3, 2)


def encode_kernel(stage, which, tile, where, *refs):
    count = 1 if which is None else 2
    blocks = refs[: 2 * count if which is None else count]
    refs = refs[len(blocks) :]
    enc, bias, cut = refs[:3]
    acc = None if stage == STAGES[0] else refs[3]
    xa, ya = refs[-2:]
    core, y = where[0], where[2]
    depth = 4 // count

    def rows(step):
        return pl.ds(pl.multiple_of(lax.rem(y + step, 4) * KB, KB), KB)

    def activate(preact, cols):
        cutoff = cut[:, cols].astype(F32) / levels
        gate = jax.nn.sigmoid((preact - cutoff) / softness)
        return (preact * gate).astype(BF16)

    def tiles(*works):
        if stage == STAGES[-1]:
            for n in range(enc.shape[1] // tile):
                for work in works:
                    work(slice(tile * n, tile * (n + 1)))
            return

        @pl.loop(0, enc.shape[1] // tile)
        def _(n):
            for work in works:
                work(pl.ds(pl.multiple_of(n * tile, tile), tile))

    def few(parts):
        def work(cols):
            pre = bias[:, cols] + sum(
                jnp.dot(
                    parts[j // depth][j % depth], enc[rows(j), cols], preferred_element_type=F32
                )
                for j in range(4)
            )
            xa[:, cols] = activate(pre, cols)

        return work

    def many(parts):
        def work(cols):
            for i in range(count):
                part = jnp.dot(
                    parts[i][...].reshape(128 * depth, KB),
                    enc[rows(stage), cols],
                    preferred_element_type=F32,
                )
                span = slice(128 * depth * i, 128 * depth * (i + 1))
                if acc is not None:
                    part = part + acc[span, cols]
                if stage == STAGES[-1]:
                    ya[span, cols] = activate(part + bias[:, cols], cols)
                else:
                    ya[span, cols] = part

        return work

    for turn in (0, 1):

        @pl.when(core == turn)
        def _(turn=turn):
            if which is None:
                tiles(few([blocks[turn]]), many([blocks[1 - turn]]))
            elif which == turn:
                tiles(few(blocks))
            else:
                tiles(many(blocks))


def encode(stage, which, where, blocks, enc, bias, cut, acc, done=()):
    lat = enc.shape[1]
    vmem = pl.BlockSpec(memory_space=pltpu.VMEM)
    args = [*blocks, enc, bias, cut]
    aliases = {}
    if acc is not None:
        args.append(acc)
        if stage != STAGES[-1]:
            aliases = {len(args): 1}
    for i, value in enumerate(done):
        args.append(value)
        aliases[len(args)] = i
    return pl.pallas_call(
        functools.partial(encode_kernel, stage, which, 256 if stage == STAGES[-1] else 512),
        in_specs=[pl.BlockSpec(memory_space=pltpu.SMEM)] + [vmem] * len(args),
        out_specs=[vmem, vmem],
        out_shape=[
            jax.ShapeDtypeStruct((128, lat), BF16),
            jax.ShapeDtypeStruct((512, lat), BF16 if stage == STAGES[-1] else F32),
        ],
        input_output_aliases=aliases,
        compiler_params=pltpu.CompilerParams(vmem_limit_bytes=VMEM_LIMIT),
        cost_estimate=LITTLE,
        name="encode",
    )(where, *args)


def split(total):
    lane = lax.broadcasted_iota(jnp.int32, total.shape, total.ndim - 1)
    high = total.astype(BF16).astype(F32)
    return jnp.where(lane < 64, high, total - high)


def joined(pair):
    return pair + pltpu.roll(pair, 64, pair.ndim - 1)


def decode_kernel(step, tile, where, xa, ya, dec, probes, keep, send0, send1, lhs):
    core = where[0]
    pick = lax.rem(where[2] + step - where[1] + 4, 4)
    lhs[pl.ds(pl.multiple_of(core * 128, 128), 128), :] = xa[...]
    lhs[pl.ds(pl.multiple_of((1 - core) * 128, 128), 128), :] = ya[pick]
    logits = split(jnp.dot(lhs[...], probes[...], preferred_element_type=F32)).astype(BF16)
    keep[:, D:] = logits[:128]
    send1[:, C:] = logits[128:]

    if step == 0:
        for i, send in enumerate((send0, send1)):

            @pl.loop(0, C // tile)
            def _(n, i=i, send=send):
                cols = pl.ds(pl.multiple_of(C * i + n * tile, tile), tile)
                out = jnp.dot(lhs[...], dec[:, cols], preferred_element_type=F32).astype(BF16)
                keep[:, cols] = out[:128]
                send[:, pl.ds(pl.multiple_of(n * tile, tile), tile)] = out[128:]

        return
    for n in range(D // tile):
        cols = slice(tile * n, tile * (n + 1))
        send, start = (send0, tile * n) if tile * n < C else (send1, tile * n - C)
        out = jnp.dot(lhs[...], dec[:, cols], preferred_element_type=F32).astype(BF16)
        keep[:, cols] = out[:128]
        send[:, start : start + tile] = out[128:]


def decode(step, where, xa, ya, dec, probes):
    lat = dec.shape[0]
    vmem = pl.BlockSpec(memory_space=pltpu.VMEM)
    return pl.pallas_call(
        functools.partial(decode_kernel, step, 1152),
        in_specs=[pl.BlockSpec(memory_space=pltpu.SMEM)] + [vmem] * 4,
        out_specs=[vmem] * 3,
        scratch_shapes=[pltpu.VMEM((256, lat), BF16)],
        out_shape=[jax.ShapeDtypeStruct((128, w), BF16) for w in (W, C, W - C)],
        compiler_params=pltpu.CompilerParams(vmem_limit_bytes=VMEM_LIMIT),
        cost_estimate=LITTLE,
        name="decode",
    )(where, xa, ya, dec, probes)


def small_call(kernel, name, outs, *args, scalars=1, scratch=()):
    vmem = pl.BlockSpec(memory_space=pltpu.VMEM)
    smem = pl.BlockSpec(memory_space=pltpu.SMEM)
    return pl.pallas_call(
        kernel,
        in_specs=[smem] * scalars + [vmem] * (len(args) - scalars),
        out_specs=[vmem] * len(outs),
        out_shape=[jax.ShapeDtypeStruct(shape, kind) for shape, kind in outs],
        scratch_shapes=list(scratch),
        compiler_params=pltpu.CompilerParams(vmem_limit_bytes=VMEM_LIMIT),
        cost_estimate=LITTLE,
        name=name,
    )(*args)


def pair_kernel(shift, a, b0, b1, *refs):
    low, high = slice(0, C), slice(C, D)
    outs = refs if shift is None else refs[1:]
    for i in range(2):
        rows = slice(64 * i, 64 * (i + 1))
        out, spot = (outs[i], slice(0, 64)) if shift is None else (outs[0], rows)
        for cols, other in ((low, b0[rows]), (high, b1[rows, :C])):
            part = a[rows, cols].astype(F32) + other.astype(F32)
            if i == shift:
                part = part + refs[0][:, cols].astype(F32)
            out[spot, cols] = part.astype(BF16)
        logits = a[rows, D:].astype(F32) + b1[rows, C:].astype(F32)
        if i == shift:
            logits = logits + refs[0][:, D:W].astype(F32)
        out[spot, D:W] = split(joined(logits)).astype(BF16)
        if shift is None:
            out[:, W:] = jnp.zeros((64, WR - W), BF16)


def pair_sum(shift, *args):
    outs = [((64, WR), BF16)] * 2 if shift is None else [((128, W), BF16)]
    kernel = functools.partial(pair_kernel, shift)
    return small_call(kernel, "pair_sum", outs, *args, scalars=0)


def first_kernel(where, a0, b0, b1, g1, g3, *outs):
    spot = where[5]
    logits = b1[:, C:].astype(F32) + sum(r[:, D:].astype(F32) for r in (a0, g1, g3))
    logits = split(joined(logits)).astype(BF16)
    for d, out in enumerate(outs):
        rows = pl.ds(pl.multiple_of(lax.rem(spot + d, 4) * 32, 32), 32)
        for cols, other in ((slice(0, C), b0[rows, :]), (slice(C, D), b1[rows, :C])):
            part = other.astype(F32) + sum(r[rows, cols].astype(F32) for r in (a0, g1, g3))
            out[:, cols] = part.astype(BF16)
        for k in range(4):
            out[:, D + 128 * k : D + 128 * (k + 1)] = logits[32 * k : 32 * (k + 1)]


def second_kernel(where, m0, g1, g2, g3, *refs):
    outs, total, wide = refs[:4], refs[4], refs[5]
    spot = where[6]

    def four(cols):
        a0, a1, a2, a3 = (r[:, cols].astype(F32) for r in (m0, g1, g2, g3))
        return (a0 + a2) + (a1 + a3)

    total[...] = four(slice(0, D))
    for k in range(4):
        cols = slice(D + 128 * k, D + 128 * (k + 1))
        l0, l1, l2, l3 = (joined(r[:, cols].astype(F32)) for r in (m0, g1, g2, g3))
        wide[32 * k : 32 * (k + 1), :] = (l0 + l2) + (l1 + l3)
    lane = lax.broadcasted_iota(jnp.int32, (8, 128), 1)
    packed = [
        jnp.where(lane < 64, wide[8 * i : 8 * i + 8, :], wide[64 + 8 * i : 72 + 8 * i, :])
        for i in range(8)
    ]
    for d, out in enumerate(outs):
        rows = pl.ds(pl.multiple_of(lax.rem(spot + d, 4) * 8, 8), 8)
        out[:, :D] = total[rows, :]
        for i in range(8):
            out[:, D + 128 * i : D + 128 * (i + 1)] = packed[i]


def third_kernel(m0, g1, g2, g3, tokens, bias, err, logits):
    def four(cols):
        a0, a1, a2, a3 = (r[:, cols] for r in (m0, g1, g2, g3))
        return (a0 + a2) + (a1 + a3)

    gap = tokens[...] - (four(slice(0, D)) + bias[...])
    err[...] = jnp.broadcast_to(jnp.sum(gap * gap, axis=1, keepdims=True) / D, err.shape)
    logits[...] = four(slice(D, W3))


def collect_kernel(*refs):
    for i, ref in enumerate(refs[:4]):
        refs[4][i] = ref[...]


def collect(parts):
    shape = (4, *parts[0].shape)
    return small_call(collect_kernel, "collect", [(shape, parts[0].dtype)], *parts, scalars=0)[0]


def settle_kernel(source, target):
    target[...] = source[...]


def settle(value):
    outs = [(value.shape, value.dtype)]
    return small_call(settle_kernel, "settle", outs, value, scalars=0)[0]


def halves_kernel(a, b, low, high):
    low[...] = a[:2]
    high[...] = b[2:]


def halves(a, b):
    shape = (2, *a.shape[1:])
    outs = [(shape, a.dtype)] * 2
    return small_call(halves_kernel, "halves", outs, a, b, scalars=0)


def rows_kernel(where, block, side1, low, high, side3, out, wide):
    core, x, y = where[0], where[1], where[2]
    start = where[5] * 32 + where[6] * 8
    even = pl.ds(pl.multiple_of(start // 16 * 16, 16), 16)
    turn = lax.rem(y - x + 4, 4)

    def put(j, value):
        wide[...] = value.astype(F32)
        rows = pl.ds(pl.multiple_of(lax.rem(start, 16), 8), 8)
        out[:, pl.ds(pl.multiple_of(lax.rem(y + j, 4) * KB, 128), KB)] = wide[rows, :]

    @pl.when(core == 0)
    def _():
        for j in range(4):
            put(j, block[j, even, :])

    @pl.when(core == 1)
    def _():
        put(0, block[turn, even, :])
        put(1, side1[turn, even, :])
        put(3, side3[turn, even, :])

        @pl.when(turn < 2)
        def _():
            put(2, low[jnp.minimum(turn, 1), even, :])

        @pl.when(turn >= 2)
        def _():
            put(2, high[jnp.maximum(turn - 2, 0), even, :])


def finish_kernel(groups, where, own, oth, labels, bias, *refs):
    actives, ya = refs[:4], refs[4]
    grad, bias_grad, loss, logits, slopes = refs[5:]
    core, x, y = where[0], where[1], where[2]
    lane = lax.broadcasted_iota(jnp.int32, (8, 128), 1)

    def unpack(source, start, parity):
        for d in range(4):
            g = lax.rem(start + d, 4) * 2 + parity
            for i in range(8):
                tile = source[d, :, 128 * i : 128 * (i + 1)]
                logits[g, 8 * i : 8 * i + 8, :] = tile
                logits[g, 64 + 8 * i : 72 + 8 * i, :] = pltpu.roll(tile, 64, 1)

    @pl.when(core == 0)
    def _():
        unpack(own, x, 0)
        unpack(oth, y, 1)

    @pl.when(core == 1)
    def _():
        unpack(oth, x, 0)
        unpack(own, y, 1)

    slopes[...] = jnp.zeros_like(slopes)
    total = jnp.zeros((128, 64), F32)
    sums = jnp.zeros((1, 64), F32)
    for g in range(groups):
        value = logits[g, :, :64] + bias[...]
        target = labels[128 * g : 128 * (g + 1), :].astype(F32)
        slope = (jax.nn.sigmoid(value) - target).astype(BF16)
        slopes[g, :, :64] = slope
        total = total + (jax.nn.softplus(value) - target * value)
        sums = sums + jnp.sum(slope.astype(F32), axis=0, keepdims=True)
    loss[...] = jnp.broadcast_to(
        jnp.sum(jnp.sum(total, axis=1, keepdims=True), axis=0, keepdims=True) / (groups * 128 * 64),
        loss.shape,
    )
    bias_grad[...] = sums / 128

    turned = jnp.zeros((128, ya.shape[2]), F32)
    for d in range(4):
        g = lax.rem(x + d, 4) * 2
        for active, slope in ((actives[d][...], slopes[g]), (ya[d], slopes[g + 1])):
            turned = turned + lax.dot_general(
                slope, active, (((0,), (0,)), ((), ())), preferred_element_type=F32
            )
    grad[...] = (turned / 128)[:64]


def on_device(
    residual, encoder, encoder_bias, thresholds, decoder, decoder_bias, probes, probe_bias, labels
):
    per_group = residual.shape[0]
    lat = encoder.shape[1]
    pos = lax.axis_index(AXES)
    core = pos % 2
    x, z, y = (pos // 2) % 4, (pos // 8) % 4, pos // 32
    is0 = core == 0
    first = jnp.where(is0, x, y)
    second = jnp.where(is0, y, z)
    third = jnp.where(is0, z, x)
    where = jnp.stack([core, x, y, z, first, second, third]).astype(jnp.int32)
    probes2 = jnp.concatenate([probes, probes], axis=1)

    parts = [residual] + [pull(residual, "z", "z", d) for d in (1, 2, 3)]
    unit = absolute(parts, z).transpose(1, 0, 2).reshape(per_group, KB)
    unit, where, probes2, encoder, decoder = lax.optimization_barrier(
        (unit, where, probes2, encoder, decoder)
    )
    unit = settle(unit)
    unit, encoder, decoder = lax.optimization_barrier((unit, encoder, decoder))
    encoder, decoder = load(encoder), load(decoder)
    pulled = [pull(unit, "y", "x", d) for d in (1, 2, 3)]
    unit, pulled, encoder, decoder = lax.optimization_barrier((unit, pulled, encoder, decoder))
    block = collect([unit, *pulled])
    other = swap(block)
    sides = {d: pull(block, "x", "y", d) for d in (1, 3)}

    cut = thresholds[None]
    bias = encoder_bias[None]
    xa = {}

    def run(stage, blocks, acc):
        xa[stage], acc = encode(stage, None, where, blocks, encoder, bias, cut, acc)
        return acc

    acc = run(0, [block, other], None)
    sides, acc = lax.optimization_barrier((sides, acc))
    low, high = halves(sides[1], sides[3])
    far = [pull(low, "x", "y", 1), pull(high, "x", "y", 3)]
    acc = run(1, [sides[1], swap(sides[1])], acc)
    acc = run(3, [sides[3], swap(sides[3])], acc)
    far, acc = lax.optimization_barrier((far, acc))
    mixed = encode(2, 0, where, far, encoder, bias, cut, acc)
    others = [swap(half) for half in far]
    xa[2], acc = encode(2, 1, where, others, encoder, bias, cut, acc, mixed)
    ya = acc.reshape(4, 128, lat)

    keep, got = {}, {}

    def part(d, left):
        keep[d], *send = decode(d, where, left, ya, decoder, probes2)
        got[d] = [swap(half) for half in send]

    part(2, xa[2])
    over = pair_sum(None, keep[2], *got[2])
    over, left1, left3 = lax.optimization_barrier((over, xa[1], xa[3]))
    through = [pull(over[0], "x", "y", 3), pull(over[1], "x", "y", 1)]
    part(1, left1)
    part(3, left3)
    through, keep[1], keep[3], left0 = lax.optimization_barrier(
        (through, keep[1], keep[3], xa[0])
    )
    (message1,) = pair_sum(0, keep[1], *got[1], through[0])
    (message3,) = pair_sum(1, keep[3], *got[3], through[1])
    message1, message3, left0 = lax.optimization_barrier((message1, message3, left0))
    part(0, left0)
    mine = {1: pull(message1, "x", "y", 3), 3: pull(message3, "x", "y", 1)}
    (tokens,) = small_call(
        rows_kernel, "own_rows", [((8, D), F32)],
        where, block, sides[1], *far, sides[3], scratch=[pltpu.VMEM((16, KB), F32)],
    )

    m2 = small_call(
        first_kernel, "first_sum", [((32, W2), BF16)] * 4,
        where, keep[0], *got[0], mine[1], mine[3],
    )
    g2 = [pull(m2[d], "y", "z", 4 - d) for d in (1, 2, 3)]
    m3 = small_call(
        second_kernel, "second_sum", [((8, W3), F32)] * 4, where, m2[0], *g2,
        scratch=[pltpu.VMEM((32, D), F32), pltpu.VMEM((128, 128), F32)],
    )
    g3 = [pull(m3[d], "z", "x", 4 - d) for d in (1, 2, 3)]
    err, packed = small_call(
        third_kernel, "third_sum", [((8, 128), F32), ((8, 1024), F32)],
        m3[0], *g3, tokens, decoder_bias[None], scalars=0,
    )
    owners = []
    for p, c in coords():
        s = (p["x"], p["y"], p["z"]) if c == 0 else (p["y"], p["z"], p["x"])
        owners.append((place(p, c), s[0] * 32 + c * 16 + s[1] * 4 + s[2]))

    pulled = [pull(packed, "x", "y", d) for d in (1, 2, 3)]
    mine = collect([packed, *pulled])
    theirs = swap(mine)
    err = lax.ppermute(err, AXES, owners)
    probe_grad, bias_grad, mean_loss = small_call(
        functools.partial(finish_kernel, 8), "finish",
        [((64, lat), F32), ((1, 64), F32), ((1, 128), F32)],
        where, mine, theirs, labels, probe_bias[None], xa[0], xa[1], xa[2], xa[3], ya,
        scratch=[pltpu.VMEM((8, 128, 128), F32), pltpu.VMEM((8, 128, 128), BF16)],
    )
    err, mean_loss = lax.optimization_barrier((err, mean_loss))
    return (err[:, 0], probe_grad.T, bias_grad[0], mean_loss[0, 0])


def solution(mesh):
    in_specs = (
        P("dp", "latent"),
        P(None, ("latent", "dp")),
        P(("latent", "dp")),
        P(("latent", "dp")),
        P(("latent", "dp"), None),
        P(),
        P(("latent", "dp"), None),
        P(),
        P(),
    )
    out_specs = (P(("latent", "dp")), P(("latent", "dp"), None), P(), P())
    return jax.shard_map(
        on_device, mesh=mesh, in_specs=in_specs, out_specs=out_specs, check_vma=False
    )
```

```python
import functools

import jax
import jax.numpy as jnp
from jax import lax
from jax.experimental import pallas as pl
from jax.experimental.pallas import tpu as pltpu
from jax.sharding import PartitionSpec as P

softness = 0.1
levels = 256.0
AXES = ("latent", "dp")
F32 = jnp.float32
BF16 = jnp.bfloat16
KB = 1152
D = 4608
W = D + 128
WR = W + 256
W2 = D + 512
C = D // 2
W3 = D + 1024
VMEM_LIMIT = 8 * 1024 * 1024
LITTLE = pl.CostEstimate(flops=1000000, bytes_accessed=0, transcendentals=0)


def flat(y, z, x, c):
    return ((y * 4 + z) * 4 + x) * 2 + c


def coords():
    for y in range(4):
        for z in range(4):
            for x in range(4):
                for c in range(2):
                    yield {"y": y, "z": z, "x": x}, c


def place(p, c):
    return flat(p["y"], p["z"], p["x"], c)


def pull_perm(axis0, axis1, step):
    pairs = []
    for p, c in coords():
        axis = (axis0, axis1)[c]
        q = dict(p)
        q[axis] = (p[axis] + step) % 4
        pairs.append((place(q, c), place(p, c)))
    return pairs


def pull(value, axis0, axis1, step):
    return lax.ppermute(value, AXES, pull_perm(axis0, axis1, step))


def swap(value):
    pairs = [(place(p, c), place(p, 1 - c)) for p, c in coords()]
    return lax.ppermute(value, AXES, pairs)


def absolute(parts, start):
    twice = jnp.stack(list(parts) * 2)
    return lax.dynamic_slice_in_dim(twice, lax.rem(4 - start, 4), 4, 0)


def load_kernel(source, target, sems):
    pieces = sems.shape[0]
    rows = source.shape[0] // pieces
    copies = []
    for i in range(pieces):
        span = slice(rows * i, rows * (i + 1))
        copies.append(pltpu.make_async_copy(source.at[span], target.at[span], sems.at[i]))
    for copy in copies:
        copy.start()
    for copy in copies:
        copy.wait()


def load(value):
    held = pl.pallas_call(
        load_kernel,
        in_specs=[pl.BlockSpec(memory_space=pltpu.HBM)],
        out_specs=pl.BlockSpec(memory_space=pltpu.VMEM),
        out_shape=jax.ShapeDtypeStruct(value.shape, value.dtype),
        scratch_shapes=[pltpu.SemaphoreType.DMA((4,))],
        compiler_params=pltpu.CompilerParams(vmem_limit_bytes=VMEM_LIMIT),
        cost_estimate=LITTLE,
        name="load",
    )(pltpu.with_memory_space_constraint(value, pltpu.HBM))
    return near(held)


def near(value):
    return pltpu.with_memory_space_constraint(value, pltpu.VMEM)


STAGES = (0, 1, 3, 2)


def encode_kernel(stage, which, tile, where, *refs):
    count = 1 if which is None else 2
    blocks = refs[: 2 * count if which is None else count]
    refs = refs[len(blocks) :]
    enc, bias, cut = refs[:3]
    acc = None if stage == STAGES[0] else refs[3]
    xa, ya = refs[-2:]
    core, y = where[0], where[2]
    depth = 4 // count

    def rows(step):
        return pl.ds(pl.multiple_of(lax.rem(y + step, 4) * KB, KB), KB)

    def activate(preact, cols):
        cutoff = cut[:, cols].astype(F32) / levels
        gate = jax.nn.sigmoid((preact - cutoff) / softness)
        return (preact * gate).astype(BF16)

    def tiles(*works):
        if stage == STAGES[-1]:
            for n in range(enc.shape[1] // tile):
                for work in works:
                    work(slice(tile * n, tile * (n + 1)))
            return

        @pl.loop(0, enc.shape[1] // tile)
        def _(n):
            for work in works:
                work(pl.ds(pl.multiple_of(n * tile, tile), tile))

    def few(parts):
        def work(cols):
            pre = bias[:, cols] + sum(
                jnp.dot(
                    parts[j // depth][j % depth], enc[rows(j), cols], preferred_element_type=F32
                )
                for j in range(4)
            )
            xa[:, cols] = activate(pre, cols)

        return work

    def many(parts):
        def work(cols):
            for i in range(count):
                part = jnp.dot(
                    parts[i][...].reshape(128 * depth, KB),
                    enc[rows(stage), cols],
                    preferred_element_type=F32,
                )
                span = slice(128 * depth * i, 128 * depth * (i + 1))
                if acc is not None:
                    part = part + acc[span, cols]
                if stage == STAGES[-1]:
                    ya[span, cols] = activate(part + bias[:, cols], cols)
                else:
                    ya[span, cols] = part

        return work

    for turn in (0, 1):

        @pl.when(core == turn)
        def _(turn=turn):
            if which is None:
                tiles(few([blocks[turn]]), many([blocks[1 - turn]]))
            elif which == turn:
                tiles(few(blocks))
            else:
                tiles(many(blocks))


def encode(stage, which, where, blocks, enc, bias, cut, acc, done=()):
    lat = enc.shape[1]
    vmem = pl.BlockSpec(memory_space=pltpu.VMEM)
    args = [*blocks, enc, bias, cut]
    aliases = {}
    if acc is not None:
        args.append(acc)
        if stage != STAGES[-1]:
            aliases = {len(args): 1}
    for i, value in enumerate(done):
        args.append(value)
        aliases[len(args)] = i
    return pl.pallas_call(
        functools.partial(encode_kernel, stage, which, 256),
        in_specs=[pl.BlockSpec(memory_space=pltpu.SMEM)] + [vmem] * len(args),
        out_specs=[vmem, vmem],
        out_shape=[
            jax.ShapeDtypeStruct((128, lat), BF16),
            jax.ShapeDtypeStruct((512, lat), BF16 if stage == STAGES[-1] else F32),
        ],
        input_output_aliases=aliases,
        compiler_params=pltpu.CompilerParams(vmem_limit_bytes=VMEM_LIMIT),
        cost_estimate=LITTLE,
        name="encode",
    )(where, *args)


def split(total):
    lane = lax.broadcasted_iota(jnp.int32, total.shape, total.ndim - 1)
    high = total.astype(BF16).astype(F32)
    return jnp.where(lane < 64, high, total - high)


def joined(pair):
    return pair + pltpu.roll(pair, 64, pair.ndim - 1)


def decode_kernel(step, tile, where, xa, ya, dec, probes, keep, send0, send1, lhs):
    core = where[0]
    pick = lax.rem(where[2] + step - where[1] + 4, 4)
    lhs[pl.ds(pl.multiple_of(core * 128, 128), 128), :] = xa[...]
    lhs[pl.ds(pl.multiple_of((1 - core) * 128, 128), 128), :] = ya[pick]
    logits = split(jnp.dot(lhs[...], probes[...], preferred_element_type=F32)).astype(BF16)
    keep[:, D:] = logits[:128]
    send1[:, C:] = logits[128:]

    if step == 0:
        for i, send in enumerate((send0, send1)):

            @pl.loop(0, C // tile)
            def _(n, i=i, send=send):
                cols = pl.ds(pl.multiple_of(C * i + n * tile, tile), tile)
                out = jnp.dot(lhs[...], dec[:, cols], preferred_element_type=F32).astype(BF16)
                keep[:, cols] = out[:128]
                send[:, pl.ds(pl.multiple_of(n * tile, tile), tile)] = out[128:]

        return
    for n in range(D // tile):
        cols = slice(tile * n, tile * (n + 1))
        send, start = (send0, tile * n) if tile * n < C else (send1, tile * n - C)
        out = jnp.dot(lhs[...], dec[:, cols], preferred_element_type=F32).astype(BF16)
        keep[:, cols] = out[:128]
        send[:, start : start + tile] = out[128:]


def decode(step, where, xa, ya, dec, probes):
    lat = dec.shape[0]
    vmem = pl.BlockSpec(memory_space=pltpu.VMEM)
    return pl.pallas_call(
        functools.partial(decode_kernel, step, 1152 if step else 256),
        in_specs=[pl.BlockSpec(memory_space=pltpu.SMEM)] + [vmem] * 4,
        out_specs=[vmem] * 3,
        scratch_shapes=[pltpu.VMEM((256, lat), BF16)],
        out_shape=[jax.ShapeDtypeStruct((128, w), BF16) for w in (W, C, W - C)],
        compiler_params=pltpu.CompilerParams(vmem_limit_bytes=VMEM_LIMIT),
        cost_estimate=LITTLE,
        name="decode",
    )(where, xa, ya, dec, probes)


def small_call(kernel, name, outs, *args, scalars=1, scratch=()):
    vmem = pl.BlockSpec(memory_space=pltpu.VMEM)
    smem = pl.BlockSpec(memory_space=pltpu.SMEM)
    return pl.pallas_call(
        kernel,
        in_specs=[smem] * scalars + [vmem] * (len(args) - scalars),
        out_specs=[vmem] * len(outs),
        out_shape=[jax.ShapeDtypeStruct(shape, kind) for shape, kind in outs],
        scratch_shapes=list(scratch),
        compiler_params=pltpu.CompilerParams(vmem_limit_bytes=VMEM_LIMIT),
        cost_estimate=LITTLE,
        name=name,
    )(*args)


def pair_kernel(shift, a, b0, b1, *refs):
    low, high = slice(0, C), slice(C, D)
    outs = refs if shift is None else refs[1:]
    for i in range(2):
        rows = slice(64 * i, 64 * (i + 1))
        out, spot = (outs[i], slice(0, 64)) if shift is None else (outs[0], rows)
        for cols, other in ((low, b0[rows]), (high, b1[rows, :C])):
            part = a[rows, cols].astype(F32) + other.astype(F32)
            if i == shift:
                part = part + refs[0][:, cols].astype(F32)
            out[spot, cols] = part.astype(BF16)
        logits = a[rows, D:].astype(F32) + b1[rows, C:].astype(F32)
        if i == shift:
            logits = logits + refs[0][:, D:W].astype(F32)
        out[spot, D:W] = split(joined(logits)).astype(BF16)
        if shift is None:
            out[:, W:] = jnp.zeros((64, WR - W), BF16)


def pair_sum(shift, *args):
    outs = [((64, WR), BF16)] * 2 if shift is None else [((128, W), BF16)]
    kernel = functools.partial(pair_kernel, shift)
    return small_call(kernel, "pair_sum", outs, *args, scalars=0)


def first_kernel(where, a0, b0, b1, g1, g3, *outs):
    spot = where[5]
    logits = b1[:, C:].astype(F32) + sum(r[:, D:].astype(F32) for r in (a0, g1, g3))
    logits = split(joined(logits)).astype(BF16)
    for d, out in enumerate(outs):
        rows = pl.ds(pl.multiple_of(lax.rem(spot + d, 4) * 32, 32), 32)
        for cols, other in ((slice(0, C), b0[rows, :]), (slice(C, D), b1[rows, :C])):
            part = other.astype(F32) + sum(r[rows, cols].astype(F32) for r in (a0, g1, g3))
            out[:, cols] = part.astype(BF16)
        for k in range(4):
            out[:, D + 128 * k : D + 128 * (k + 1)] = logits[32 * k : 32 * (k + 1)]


def second_kernel(where, m0, g1, g2, g3, *refs):
    outs, total, wide = refs[:4], refs[4], refs[5]
    spot = where[6]

    def four(cols):
        a0, a1, a2, a3 = (r[:, cols].astype(F32) for r in (m0, g1, g2, g3))
        return (a0 + a2) + (a1 + a3)

    total[...] = four(slice(0, D))
    for k in range(4):
        cols = slice(D + 128 * k, D + 128 * (k + 1))
        l0, l1, l2, l3 = (joined(r[:, cols].astype(F32)) for r in (m0, g1, g2, g3))
        wide[32 * k : 32 * (k + 1), :] = (l0 + l2) + (l1 + l3)
    lane = lax.broadcasted_iota(jnp.int32, (8, 128), 1)
    packed = [
        jnp.where(lane < 64, wide[8 * i : 8 * i + 8, :], wide[64 + 8 * i : 72 + 8 * i, :])
        for i in range(8)
    ]
    for d, out in enumerate(outs):
        rows = pl.ds(pl.multiple_of(lax.rem(spot + d, 4) * 8, 8), 8)
        out[:, :D] = total[rows, :]
        for i in range(8):
            out[:, D + 128 * i : D + 128 * (i + 1)] = packed[i]


def third_kernel(m0, g1, g2, g3, tokens, bias, err, logits):
    def four(cols):
        a0, a1, a2, a3 = (r[:, cols] for r in (m0, g1, g2, g3))
        return (a0 + a2) + (a1 + a3)

    gap = tokens[...] - (four(slice(0, D)) + bias[...])
    err[...] = jnp.broadcast_to(jnp.sum(gap * gap, axis=1, keepdims=True) / D, err.shape)
    logits[...] = four(slice(D, W3))


def collect_kernel(*refs):
    for i, ref in enumerate(refs[:4]):
        refs[4][i] = ref[...]


def collect(parts):
    shape = (4, *parts[0].shape)
    return small_call(collect_kernel, "collect", [(shape, parts[0].dtype)], *parts, scalars=0)[0]


def settle_kernel(source, target):
    target[...] = source[...]


def settle(value):
    outs = [(value.shape, value.dtype)]
    return small_call(settle_kernel, "settle", outs, value, scalars=0)[0]


def halves_kernel(a, b, low, high):
    low[...] = a[:2]
    high[...] = b[2:]


def halves(a, b):
    shape = (2, *a.shape[1:])
    outs = [(shape, a.dtype)] * 2
    return small_call(halves_kernel, "halves", outs, a, b, scalars=0)


def rows_kernel(where, block, side1, low, high, side3, out, wide):
    core, x, y = where[0], where[1], where[2]
    start = where[5] * 32 + where[6] * 8
    even = pl.ds(pl.multiple_of(start // 16 * 16, 16), 16)
    turn = lax.rem(y - x + 4, 4)

    def put(j, value):
        wide[...] = value.astype(F32)
        rows = pl.ds(pl.multiple_of(lax.rem(start, 16), 8), 8)
        out[:, pl.ds(pl.multiple_of(lax.rem(y + j, 4) * KB, 128), KB)] = wide[rows, :]

    @pl.when(core == 0)
    def _():
        for j in range(4):
            put(j, block[j, even, :])

    @pl.when(core == 1)
    def _():
        put(0, block[turn, even, :])
        put(1, side1[turn, even, :])
        put(3, side3[turn, even, :])

        @pl.when(turn < 2)
        def _():
            put(2, low[jnp.minimum(turn, 1), even, :])

        @pl.when(turn >= 2)
        def _():
            put(2, high[jnp.maximum(turn - 2, 0), even, :])


def finish_kernel(groups, where, own, oth, labels, bias, *refs):
    actives, ya = refs[:4], refs[4]
    grad, bias_grad, loss, logits, slopes = refs[5:]
    core, x, y = where[0], where[1], where[2]
    lane = lax.broadcasted_iota(jnp.int32, (8, 128), 1)

    def unpack(source, start, parity):
        for d in range(4):
            g = lax.rem(start + d, 4) * 2 + parity
            for i in range(8):
                tile = source[d, :, 128 * i : 128 * (i + 1)]
                logits[g, 8 * i : 8 * i + 8, :] = tile
                logits[g, 64 + 8 * i : 72 + 8 * i, :] = pltpu.roll(tile, 64, 1)

    @pl.when(core == 0)
    def _():
        unpack(own, x, 0)
        unpack(oth, y, 1)

    @pl.when(core == 1)
    def _():
        unpack(oth, x, 0)
        unpack(own, y, 1)

    slopes[...] = jnp.zeros_like(slopes)
    total = jnp.zeros((128, 64), F32)
    sums = jnp.zeros((1, 64), F32)
    for g in range(groups):
        value = logits[g, :, :64] + bias[...]
        target = labels[128 * g : 128 * (g + 1), :].astype(F32)
        slope = (jax.nn.sigmoid(value) - target).astype(BF16)
        slopes[g, :, :64] = slope
        total = total + (jax.nn.softplus(value) - target * value)
        sums = sums + jnp.sum(slope.astype(F32), axis=0, keepdims=True)
    loss[...] = jnp.broadcast_to(
        jnp.sum(jnp.sum(total, axis=1, keepdims=True), axis=0, keepdims=True) / (groups * 128 * 64),
        loss.shape,
    )
    bias_grad[...] = sums / 128

    turned = jnp.zeros((128, ya.shape[2]), F32)
    for d in range(4):
        g = lax.rem(x + d, 4) * 2
        for active, slope in ((actives[d][...], slopes[g]), (ya[d], slopes[g + 1])):
            turned = turned + lax.dot_general(
                slope, active, (((0,), (0,)), ((), ())), preferred_element_type=F32
            )
    grad[...] = (turned / 128)[:64]


def on_device(
    residual, encoder, encoder_bias, thresholds, decoder, decoder_bias, probes, probe_bias, labels
):
    per_group = residual.shape[0]
    lat = encoder.shape[1]
    pos = lax.axis_index(AXES)
    core = pos % 2
    x, z, y = (pos // 2) % 4, (pos // 8) % 4, pos // 32
    is0 = core == 0
    first = jnp.where(is0, x, y)
    second = jnp.where(is0, y, z)
    third = jnp.where(is0, z, x)
    where = jnp.stack([core, x, y, z, first, second, third]).astype(jnp.int32)
    probes2 = jnp.concatenate([probes, probes], axis=1)

    parts = [residual] + [pull(residual, "z", "z", d) for d in (1, 2, 3)]
    unit = absolute(parts, z).transpose(1, 0, 2).reshape(per_group, KB)
    unit, where, probes2, encoder, decoder = lax.optimization_barrier(
        (unit, where, probes2, encoder, decoder)
    )
    unit = settle(unit)
    unit, encoder, decoder = lax.optimization_barrier((unit, encoder, decoder))
    encoder, decoder = load(encoder), load(decoder)
    pulled = [pull(unit, "y", "x", d) for d in (1, 2, 3)]
    unit, pulled, encoder, decoder = lax.optimization_barrier((unit, pulled, encoder, decoder))
    block = collect([unit, *pulled])
    other = swap(block)
    sides = {d: pull(block, "x", "y", d) for d in (1, 3)}

    cut = thresholds[None]
    bias = encoder_bias[None]
    xa = {}

    def run(stage, blocks, acc):
        xa[stage], acc = encode(stage, None, where, blocks, encoder, bias, cut, acc)
        return acc

    acc = run(0, [block, other], None)
    sides, acc = lax.optimization_barrier((sides, acc))
    low, high = halves(sides[1], sides[3])
    far = [pull(low, "x", "y", 1), pull(high, "x", "y", 3)]
    acc = run(1, [sides[1], swap(sides[1])], acc)
    acc = run(3, [sides[3], swap(sides[3])], acc)
    far, acc = lax.optimization_barrier((far, acc))
    mixed = encode(2, 0, where, far, encoder, bias, cut, acc)
    others = [swap(half) for half in far]
    xa[2], acc = encode(2, 1, where, others, encoder, bias, cut, acc, mixed)
    ya = acc.reshape(4, 128, lat)

    keep, got = {}, {}

    def part(d, left):
        keep[d], *send = decode(d, where, left, ya, decoder, probes2)
        got[d] = [swap(half) for half in send]

    part(2, xa[2])
    over = pair_sum(None, keep[2], *got[2])
    over, left1, left3 = lax.optimization_barrier((over, xa[1], xa[3]))
    through = [pull(over[0], "x", "y", 3), pull(over[1], "x", "y", 1)]
    part(1, left1)
    part(3, left3)
    through, keep[1], keep[3], left0 = lax.optimization_barrier(
        (through, keep[1], keep[3], xa[0])
    )
    (message1,) = pair_sum(0, keep[1], *got[1], through[0])
    (message3,) = pair_sum(1, keep[3], *got[3], through[1])
    message1, message3, left0 = lax.optimization_barrier((message1, message3, left0))
    part(0, left0)
    mine = {1: pull(message1, "x", "y", 3), 3: pull(message3, "x", "y", 1)}
    (tokens,) = small_call(
        rows_kernel, "own_rows", [((8, D), F32)],
        where, block, sides[1], *far, sides[3], scratch=[pltpu.VMEM((16, KB), F32)],
    )

    m2 = small_call(
        first_kernel, "first_sum", [((32, W2), BF16)] * 4,
        where, keep[0], *got[0], mine[1], mine[3],
    )
    g2 = [pull(m2[d], "y", "z", 4 - d) for d in (1, 2, 3)]
    m3 = small_call(
        second_kernel, "second_sum", [((8, W3), F32)] * 4, where, m2[0], *g2,
        scratch=[pltpu.VMEM((32, D), F32), pltpu.VMEM((128, 128), F32)],
    )
    g3 = [pull(m3[d], "z", "x", 4 - d) for d in (1, 2, 3)]
    err, packed = small_call(
        third_kernel, "third_sum", [((8, 128), F32), ((8, 1024), F32)],
        m3[0], *g3, tokens, decoder_bias[None], scalars=0,
    )
    owners = []
    for p, c in coords():
        s = (p["x"], p["y"], p["z"]) if c == 0 else (p["y"], p["z"], p["x"])
        owners.append((place(p, c), s[0] * 32 + c * 16 + s[1] * 4 + s[2]))

    pulled = [pull(packed, "x", "y", d) for d in (1, 2, 3)]
    mine = collect([packed, *pulled])
    theirs = swap(mine)
    err = lax.ppermute(err, AXES, owners)
    probe_grad, bias_grad, mean_loss = small_call(
        functools.partial(finish_kernel, 8), "finish",
        [((64, lat), F32), ((1, 64), F32), ((1, 128), F32)],
        where, mine, theirs, labels, probe_bias[None], xa[0], xa[1], xa[2], xa[3], ya,
        scratch=[pltpu.VMEM((8, 128, 128), F32), pltpu.VMEM((8, 128, 128), BF16)],
    )
    err, mean_loss = lax.optimization_barrier((err, mean_loss))
    return (err[:, 0], probe_grad.T, bias_grad[0], mean_loss[0, 0])


def solution(mesh):
    in_specs = (
        P("dp", "latent"),
        P(None, ("latent", "dp")),
        P(("latent", "dp")),
        P(("latent", "dp")),
        P(("latent", "dp"), None),
        P(),
        P(("latent", "dp"), None),
        P(),
        P(),
    )
    out_specs = (P(("latent", "dp")), P(("latent", "dp"), None), P(), P())
    return jax.shard_map(
        on_device, mesh=mesh, in_specs=in_specs, out_specs=out_specs, check_vma=False
    )
```
